128 devices in a mesh: macro: 4 (over y), rve: 32 (over z, x, core).
Axes of the slice: x: 4, y: 4, z: 4, core: 2. Of those that a mesh axis runs over, the one named last changes fastest.
Arguments:
- displacement: float32 [3, 128, 8, 16], P(None, ('macro', 'rve')), may hold values from -1.5 to 1.5
- velocity: float32 [3, 128, 8, 16], P(None, ('macro', 'rve')), may hold values from -3 to 3
- old_owner: int32 [16384, 1], P(('macro', 'rve')), may hold values from 0 to 31; in each aligned block of 128 rows (0 to 127, 128 to 255, ...) at most 8 rows name the same one
- new_owner: int32 [16384, 1], P(('macro', 'rve')), may hold values from 0 to 31; in each aligned block of 128 rows (0 to 127, 128 to 255, ...) at most 8 rows name the same one
- substeps: int32 [16384], P(('macro', 'rve')), may hold values from 1 to 8
- strut_ends: int32 [2, 4096], replicated, may hold values from 0 to 511, as said below
- flow_stress: float32 [4096], replicated, may hold values from 0.2 to 2
- relax_rate: float32 [4096], replicated, may hold values from 0.02 to 0.3
- plastic_old: float32 [32768, 4096], P(('macro', 'rve')), may hold values from -0.5 to 0.5
Outputs:
- displacement_next: float32 [3, 128, 8, 16], P(None, ('macro', 'rve'))
- velocity_next: float32 [3, 128, 8, 16], P(None, ('macro', 'rve'))
- plastic_new: float32 [32768, 4096], P(('macro', 'rve'))
The draws below stay inside these ranges and needn't reach their ends.
Inputs may be any that keep to these rules, and one draw needn't show every extreme that they name: `old_owner`: the elements of one device name one owner at most 8 times, a bound that some block reaches. `new_owner`: the elements of one device name one owner at most 8 times, a bound that some block reaches. `strut_ends`: the two nodes of a strut are distinct and their lattice coordinates differ by at most one along each dimension, modulo 8.
All inputs are finite; a program needn't handle non-finite values.
Results may differ from the reference program's by a relative error of at most 0.0003.
Values sent between devices are 32-bit elements; how exact they have to be, the bound alone decides.
No kernel may reach another device: no remote copies, remote signals or barrier semaphores. Data moves between devices by JAX's collectives and lax.ppermute only.
A program may use at most 64 MiB of HBM per device.

```python
import math
import jax
import jax.numpy as jnp
import numpy as np
from jax import lax

EY = 8
EZ = 16
STRUTS = 4096
NSUB = 8
LATTICE = 8
POINTS_DEV = 128
CAP = 8
NX = 128
NPTS = 16384
SLOTS = 32768
N_MACRO = 4
N_RVE = 32


def draw_strut_ends(key, part):
    key = jax.random.fold_in(key, 11)
    first_key, second_key = jax.random.split(key)
    lattice_side = LATTICE
    node_first = jax.random.randint(first_key, (STRUTS,), 0, lattice_side * lattice_side * lattice_side)
    direction_pick = jax.random.randint(second_key, (STRUTS,), 0, 26)
    direction_pick = direction_pick + (direction_pick >= 13).astype(jnp.int32)
    move_plane = direction_pick // 9 - 1
    move_row = direction_pick // 3 % 3 - 1
    move_col = direction_pick % 3 - 1
    plane_pos = node_first // (lattice_side * lattice_side)
    row_pos = node_first // lattice_side % lattice_side
    col_pos = node_first % lattice_side
    node_second = (plane_pos + move_plane) % lattice_side * lattice_side * lattice_side + (row_pos + move_row) % lattice_side * lattice_side + (col_pos + move_col) % lattice_side
    return jnp.stack([node_first, node_second]).astype(jnp.int32)


def touch_ends(values, rng, least, high):
    longest = values.shape.index(max(values.shape))
    spots = []
    for shift in (0, 1):
        where = [jax.random.randint(jax.random.fold_in(rng, axis), (), 0, length) for axis, length in enumerate(values.shape)]
        where[longest] = (where[longest] + shift) % values.shape[longest]
        spots.append(tuple(where))
    return values.at[spots[0]].set(least).at[spots[1]].set(high)


def block_levels(own_key, extent, cuts, least, top_value):
    loudness = 1.0
    for position, parts in cuts:
        draws = jax.random.uniform(jax.random.fold_in(jax.random.fold_in(own_key, 6), position), (parts,), jnp.float32, least / len(cuts), top_value / len(cuts))
        loudness = loudness * jnp.repeat(jnp.exp(draws), extent[position] // parts).reshape((-1,) + (1,) * (len(extent) - 1 - position))
    return loudness


def routed_block(rng, own, number, rows, count, top, limit, skew):
    sequence = jax.random.permutation(rng, count)
    crowded, common = load_shares(count, rows * top, limit, skew, True), load_shares(count, rows * top, limit, skew, False)
    places = jnp.arange(count)

    def named(tallies, rotation):
        used = int((tallies > 0).sum())
        fixed = max(1, used // 4)
        moved = fixed + (places - fixed + rotation * (used - fixed)) % max(1, count - fixed)
        return jnp.zeros((count,), jnp.int32).at[sequence[jnp.where(places < fixed, places, moved)]].set(jnp.asarray(tallies, jnp.int32))

    tallies = jnp.where(number % 4 == 0, named(crowded, number // 4), named(common, number - number // 4 - 1))
    mixed = jax.random.permutation(jax.random.fold_in(own, 3), count)
    donor, receiver = mixed[0:count // 2 * 2:2], mixed[1:count // 2 * 2:2]
    room = jnp.minimum(tallies[donor] - 1, limit - tallies[receiver]) // 2
    room = jnp.where((donor == sequence[0]) | (receiver == sequence[0]) | (tallies[receiver] == 0), 0, jnp.maximum(room, 0))
    moved = jax.random.randint(jax.random.fold_in(own, 4), (count // 2,), 0, 1 << 20) % (room + 1)
    tallies = tallies.at[donor].add(-moved).at[receiver].add(moved)
    items = jnp.searchsorted(jnp.cumsum(tallies), jnp.arange(rows * top), side="right").astype(jnp.int32)
    listing = items.reshape(top, rows).T
    listing = listing[jax.random.permutation(jax.random.fold_in(own, 1), rows)]
    rotation = jax.random.randint(jax.random.fold_in(own, 2), (rows, 1), 0, top)
    return jnp.take_along_axis(listing, (jnp.arange(top)[None, :] + rotation) % top, axis=1)


def load_shares(count, total, most, slope, full):
    weights = [(1 << 20) // math.isqrt(rank ** slope) + 1 for rank in range(1, count + 1)]
    largest = most if full else min(most, max(-(-total // count), total * weights[0] // sum(weights)))
    least = 1 if total - largest >= count - 1 else 0
    holding, surplus = [largest] + [least] * (count - 1), total - largest - least * (count - 1)
    while surplus > 0:
        candidates = [i for i in range(1, count) if holding[i] < largest] or [i for i in range(1, count) if holding[i] < most]
        whole, remaining = sum([weights[i] for i in candidates]), surplus
        for i in candidates:
            more = min(most - holding[i], max(1, remaining * weights[i] // whole), surplus)
            holding[i] = holding[i] + more
            surplus = surplus - more
    return np.array(holding)


def bell_draw(rng, dims, deviation, limit, shards=(), kind=jnp.bfloat16):
    loudness = block_levels(rng, dims, shards, -0.22, 0.18) if shards else 1.0
    entries = jax.random.normal(rng, dims, jnp.float32) * deviation * loudness
    return jnp.minimum(jnp.maximum(entries, -limit), limit).astype(kind)


def setup_inputs(seed: int = 0) -> dict:
    splits = jax.random.split(jax.random.key(seed), 10)
    displacement = bell_draw(splits[0], (3, NX, EY, EZ), 0.3, 1.5, ((1, 128),), jnp.float32)
    velocity = bell_draw(splits[1], (3, NX, EY, EZ), 0.5, 3.0, ((1, 128),), jnp.float32)
    old_owner_keys = jax.random.split(jax.random.fold_in(splits[2], 1), NPTS // POINTS_DEV)
    old_owner_turns = jax.random.permutation(jax.random.fold_in(splits[2], 3), NPTS // POINTS_DEV)
    old_owner = jax.vmap(lambda own, number: routed_block(jax.random.fold_in(splits[2], 2), own, number, POINTS_DEV, N_RVE, 1, CAP, 2))(old_owner_keys, old_owner_turns).reshape((NPTS, 1))
    new_owner_keys = jax.random.split(jax.random.fold_in(splits[3], 1), NPTS // POINTS_DEV)
    new_owner_turns = jax.random.permutation(jax.random.fold_in(splits[3], 3), NPTS // POINTS_DEV)
    new_owner = jax.vmap(lambda own, number: routed_block(jax.random.fold_in(splits[3], 2), own, number, POINTS_DEV, N_RVE, 1, CAP, 2))(new_owner_keys, new_owner_turns).reshape((NPTS, 1))
    substeps = touch_ends(jax.random.randint(splits[4], (NPTS,), 1, NSUB + 1), jax.random.fold_in(splits[4], 1), 1, NSUB).astype(jnp.int32)
    strut_ends = draw_strut_ends(jax.random.fold_in(splits[9], 71), 0)
    flow_stress = jnp.clip(jnp.exp(jax.random.uniform(splits[6], (STRUTS,), jnp.float32, math.log(0.2), math.log(2.0))), 0.2, 2.0)
    relax_rate = jnp.clip(jnp.exp(jax.random.uniform(splits[7], (STRUTS,), jnp.float32, math.log(0.02), math.log(0.3))), 0.02, 0.3)
    plastic_old = jnp.clip(jax.random.uniform(splits[8], (SLOTS, STRUTS), jnp.float32, -0.5, 0.5) * block_levels(splits[8], (SLOTS, STRUTS), ((0, 128),), -0.4, 0.0), -0.5, 0.5)
    return dict(displacement=displacement, velocity=velocity, old_owner=old_owner, new_owner=new_owner, substeps=substeps, strut_ends=strut_ends, flow_stress=flow_stress, relax_rate=relax_rate, plastic_old=plastic_old)


young = 10.0
harden = 1.0
time_step = 0.2
highest = lax.Precision.HIGHEST

def lattice_coords(node_ids):
    lattice_side = LATTICE
    return jnp.stack([node_ids // (lattice_side * lattice_side), node_ids // lattice_side % lattice_side, node_ids % lattice_side])

def strut_basis(strut_ends):
    offset = lattice_coords(strut_ends[1]) - lattice_coords(strut_ends[0])
    offset = (offset + LATTICE // 2) % LATTICE - LATTICE // 2
    vector = offset.astype(jnp.float32)
    length = jnp.sqrt(lax.optimization_barrier(jnp.sum(vector * vector, axis=0)))
    direction = vector / length
    dir_x, dir_y, dir_z = (direction[0], direction[1], direction[2])
    strain_basis = jnp.stack([dir_x * dir_x, dir_y * dir_y, dir_z * dir_z, 2.0 * dir_x * dir_y, 2.0 * dir_x * dir_z, 2.0 * dir_y * dir_z])
    stress_basis = jnp.stack([dir_x * dir_x, dir_y * dir_y, dir_z * dir_z, dir_x * dir_y, dir_x * dir_z, dir_y * dir_z]) / STRUTS
    return (strain_basis, stress_basis)

def green(deform):

    def column_dot(col_a, col_b):
        return deform[col_a] * deform[col_b] + deform[3 + col_a] * deform[3 + col_b] + deform[6 + col_a] * deform[6 + col_b]
    return 0.5 * jnp.stack([column_dot(0, 0) - 1.0, column_dot(1, 1) - 1.0, column_dot(2, 2) - 1.0, column_dot(0, 1), column_dot(0, 2), column_dot(1, 2)])

def relax(deform_old, deform_new, counts, plastic, flow_stress, relax_rate, strain_basis):
    step_count = jnp.maximum(counts, 1.0)
    change = deform_new - deform_old
    rate_step = relax_rate[None, :] / step_count[:, None]
    factor = rate_step / (1.0 + (young + harden) * rate_step)

    def advance(turn_index, plastic):
        turn_level = (turn_index + 1).astype(counts.dtype)
        deform = deform_old + (turn_level / step_count)[None, :] * change
        strain = jnp.einsum('cr,cs->rs', green(deform), strain_basis, precision=highest)
        trial_stress = young * (strain - plastic) - harden * plastic
        excess = jnp.maximum(jnp.abs(trial_stress) - flow_stress[None, :], 0.0)
        active_mask = (turn_level <= counts)[:, None]
        return plastic + jnp.where(active_mask, excess * factor * jnp.sign(trial_stress), 0.0)
    return lax.fori_loop(0, NSUB, advance, plastic)

def homogenize(deform_new, plastic, strain_basis, stress_basis):
    strain = jnp.einsum('cr,cs->rs', green(deform_new), strain_basis, precision=highest)
    strut_stress = young * (strain - plastic)
    return jnp.einsum('rs,cs->cr', strut_stress, stress_basis, precision=highest)

def first_stress(deform, stress):
    pairing = ((0, 3, 4), (3, 1, 5), (4, 5, 2))
    components = []
    for row_axis in range(3):
        for col_axis in range(3):
            components.append(deform[3 * row_axis] * stress[pairing[0][col_axis]] + deform[3 * row_axis + 1] * stress[pairing[1][col_axis]] + deform[3 * row_axis + 2] * stress[pairing[2][col_axis]])
    return jnp.stack(components)

def element_deform(extended):
    plane_low = extended[:, :-1]
    plane_high = extended[:, 1:]

    def roll_second(values):
        return jnp.roll(values, -1, axis=2)

    def roll_third(values):
        return jnp.roll(values, -1, axis=3)
    diff_first = plane_high - plane_low
    slope_first = 0.25 * (diff_first + roll_second(diff_first) + roll_third(diff_first) + roll_second(roll_third(diff_first)))
    plane_mid = 0.5 * (plane_low + plane_high)
    diff_second = roll_second(plane_mid) - plane_mid
    slope_second = 0.5 * (diff_second + roll_third(diff_second))
    diff_third = roll_third(plane_mid) - plane_mid
    slope_third = 0.5 * (diff_third + roll_second(diff_third))
    slopes = jnp.stack([slope_first, slope_second, slope_third], axis=1)
    identity = jnp.eye(3, dtype=extended.dtype)
    slopes = slopes + identity[:, :, None, None, None]
    return slopes.reshape(9, -1)

def nodal_force(piola, layout):
    tensor = piola.reshape((3, 3) + layout)
    planes = layout[0]
    nodal = jnp.zeros((3, planes + 1, layout[1], layout[2]), piola.dtype)
    for offset_plane in (0, 1):
        for offset_row in (0, 1):
            for offset_col in (0, 1):
                corner_term = 0.25 * ((2 * offset_plane - 1) * tensor[:, 0] + (2 * offset_row - 1) * tensor[:, 1] + (2 * offset_col - 1) * tensor[:, 2])
                corner_term = jnp.roll(jnp.roll(corner_term, offset_row, axis=2), offset_col, axis=3)
                nodal = nodal.at[:, offset_plane:offset_plane + planes].add(corner_term)
    return nodal

def ranks(owner_map, owner_count):
    one_hot = (owner_map[:, :, None] == jnp.arange(owner_count, dtype=jnp.int32)).astype(jnp.int32)
    earlier = jnp.cumsum(one_hot, axis=1) - one_hot
    return lax.optimization_barrier(jnp.sum(earlier * one_hot, axis=2))

def reference(displacement, velocity, old_owner, new_owner, substeps, strut_ends, flow_stress, relax_rate, plastic_old):
    strain_basis, stress_basis = strut_basis(strut_ends)
    displacement_next = displacement + time_step * velocity
    zero_plane = jnp.zeros_like(displacement[:, :1])
    deform_old = element_deform(jnp.concatenate([displacement, zero_plane], axis=1))
    deform_new = element_deform(jnp.concatenate([displacement_next, zero_plane], axis=1))
    block_count = N_MACRO * N_RVE
    old_map = old_owner.reshape(block_count, POINTS_DEV)
    new_map = new_owner.reshape(block_count, POINTS_DEV)
    device_ids = jnp.arange(block_count, dtype=jnp.int32)[:, None]
    macro_row = device_ids // N_RVE
    source = device_ids % N_RVE
    old_slots = (((macro_row * N_RVE + old_map) * N_RVE + source) * CAP + ranks(old_map, N_RVE)).reshape(-1)
    new_slots = (((macro_row * N_RVE + new_map) * N_RVE + source) * CAP + ranks(new_map, N_RVE)).reshape(-1)
    gathered = plastic_old[old_slots].reshape(block_count, POINTS_DEV, STRUTS)
    counts = substeps.astype(jnp.float32).reshape(block_count, POINTS_DEV)
    old_blocks = deform_old.reshape(9, block_count, POINTS_DEV).transpose(1, 0, 2)
    new_blocks = deform_new.reshape(9, block_count, POINTS_DEV).transpose(1, 0, 2)

    def relax_block(members):
        return relax(members[0], members[1], members[2], members[3], flow_stress, relax_rate, strain_basis)
    updated = lax.map(relax_block, (old_blocks, new_blocks, counts, gathered))
    plastic_points = updated.reshape(-1, STRUTS)
    plastic_new = jnp.zeros_like(plastic_old).at[new_slots].set(plastic_points)
    stress = homogenize(deform_new, plastic_points, strain_basis, stress_basis)
    piola = first_stress(deform_new, stress)
    nodal = nodal_force(piola, (NX, EY, EZ))
    velocity_next = velocity - time_step * nodal[:, :NX]
    return (displacement_next, velocity_next, plastic_new)
```

```python
import functools

import jax
import jax.numpy as jnp
import numpy as np
from jax import lax
from jax.experimental import pallas as pl
from jax.experimental.pallas import tpu as pltpu
from jax.sharding import PartitionSpec as P

STRUTS = 4096
NSUB = 8
LATTICE = 8
LANES = 128
POINTS = 128
TILES = STRUTS // LANES
QUADS = TILES // 8

young = 10.0
harden = 1.0
time_step = 0.2
highest = lax.Precision.HIGHEST


def from_behind(value, axis, steps):
    count = lax.axis_size(axis)
    initial, last = (max(0, -steps), min(count, count - steps))
    return lax.ppermute(value, axis, [(source, source + steps) for source in range(initial, last)])


def direction_products():
    table = np.zeros((6, LANES), np.float32)
    for code in range(27):
        vector = np.array([code // 9 - 1, code // 3 % 3 - 1, code % 3 - 1], np.float32)
        length = np.sqrt(np.sum(vector * vector, dtype=np.float32))
        if length == 0:
            continue
        x, y, z = vector / length
        table[:, code] = [x * x, y * y, z * z, x * y, x * z, y * z]
    return table


def direction_codes(strut_ends):
    first, second = strut_ends[0], strut_ends[1]

    def step(scale):
        offset = second // scale % LATTICE - first // scale % LATTICE
        return (offset + LATTICE // 2) % LATTICE - LATTICE // 2

    code = (step(LATTICE * LATTICE) + 1) * 9 + (step(LATTICE) + 1) * 3 + (step(1) + 1)
    return code.reshape(TILES, LANES)


def green(deform):

    def column_dot(col_a, col_b):
        return (
            deform[col_a] * deform[col_b]
            + deform[3 + col_a] * deform[3 + col_b]
            + deform[6 + col_a] * deform[6 + col_b]
        )

    return 0.5 * jnp.stack(
        [
            column_dot(0, 0) - 1.0,
            column_dot(1, 1) - 1.0,
            column_dot(2, 2) - 1.0,
            column_dot(0, 1),
            column_dot(0, 2),
            column_dot(1, 2),
        ]
    )


def first_stress(deform, stress):
    pairing = ((0, 3, 4), (3, 1, 5), (4, 5, 2))
    components = []
    for row_axis in range(3):
        for col_axis in range(3):
            components.append(
                deform[3 * row_axis] * stress[pairing[0][col_axis]]
                + deform[3 * row_axis + 1] * stress[pairing[1][col_axis]]
                + deform[3 * row_axis + 2] * stress[pairing[2][col_axis]]
            )
    return jnp.stack(components)


def element_deform(extended):
    plane_low = extended[:, :-1]
    plane_high = extended[:, 1:]

    def roll_second(values):
        return jnp.roll(values, -1, axis=2)

    def roll_third(values):
        return jnp.roll(values, -1, axis=3)

    diff_first = plane_high - plane_low
    slope_first = 0.25 * (
        diff_first
        + roll_second(diff_first)
        + roll_third(diff_first)
        + roll_second(roll_third(diff_first))
    )
    plane_mid = 0.5 * (plane_low + plane_high)
    diff_second = roll_second(plane_mid) - plane_mid
    slope_second = 0.5 * (diff_second + roll_third(diff_second))
    diff_third = roll_third(plane_mid) - plane_mid
    slope_third = 0.5 * (diff_third + roll_second(diff_third))
    slopes = jnp.stack([slope_first, slope_second, slope_third], axis=1)
    identity = jnp.eye(3, dtype=extended.dtype)
    slopes = slopes + identity[:, :, None, None, None]
    return slopes.reshape(9, -1)


def nodal_force(piola, layout):
    tensor = piola.reshape((3, 3) + layout)
    planes = layout[0]
    nodal = jnp.zeros((3, planes + 1, layout[1], layout[2]), piola.dtype)
    for offset_plane in (0, 1):
        for offset_row in (0, 1):
            for offset_col in (0, 1):
                corner_term = 0.25 * (
                    (2 * offset_plane - 1) * tensor[:, 0]
                    + (2 * offset_row - 1) * tensor[:, 1]
                    + (2 * offset_col - 1) * tensor[:, 2]
                )
                corner_term = jnp.roll(
                    jnp.roll(corner_term, offset_row, axis=2), offset_col, axis=3
                )
                nodal = nodal.at[:, offset_plane : offset_plane + planes].add(corner_term)
    return nodal


def plan_kernel(old_ref, new_ref, steps_ref, source_ref, target_ref, order_ref, fill_ref, seen_ref):
    def clear(index, carry):
        seen_ref[index] = 0
        seen_ref[32 + index] = 0
        return carry

    lax.fori_loop(0, 32, clear, 0)

    def empty(index, carry):
        fill_ref[index] = 0
        return carry

    lax.fori_loop(0, NSUB, empty, 0)

    def place(element, carry):
        old = old_ref[element]
        rank = seen_ref[old]
        seen_ref[old] = rank + 1
        source_ref[element] = old * (8 * TILES) + rank
        new = new_ref[element]
        rank = seen_ref[32 + new]
        seen_ref[32 + new] = rank + 1
        target_ref[element] = new * (8 * TILES) + rank
        level = steps_ref[element] - 1
        position = fill_ref[level]
        fill_ref[level] = position + 1
        order_ref[level * POINTS + position] = element
        return carry

    lax.fori_loop(0, POINTS, place, 0)


def plan(old_owner, new_owner, substeps):
    smem = pl.BlockSpec(memory_space=pltpu.SMEM)
    return pl.pallas_call(
        plan_kernel,
        out_shape=(
            jax.ShapeDtypeStruct((POINTS,), jnp.int32),
            jax.ShapeDtypeStruct((POINTS,), jnp.int32),
            jax.ShapeDtypeStruct((NSUB * POINTS,), jnp.int32),
            jax.ShapeDtypeStruct((NSUB,), jnp.int32),
        ),
        in_specs=[smem] * 3,
        out_specs=(smem,) * 4,
        scratch_shapes=[pltpu.SMEM((64,), jnp.int32)],
        name="plan",
    )(old_owner, new_owner, substeps)


def row_part(start, quad):
    return pl.ds(start + 64 * quad, 8, stride=8)


def relax_kernel(
    source_ref,
    target_ref,
    order_ref,
    fill_ref,
    codes_ref,
    flow_ref,
    rate_ref,
    levels_ref,
    held_ref,
    sent_ref,
):
    sent_ref[...] = jnp.zeros_like(sent_ref)
    for steps in range(1, NSUB + 1):
        count = fill_ref[steps - 1]
        gains = []
        for quad in range(QUADS):
            rate = rate_ref[pl.ds(8 * quad, 8), :] * ((young + harden) / steps)
            gains.append(rate / (1.0 + rate))

        def pair(turn, carry, steps=steps, count=count, gains=gains):
            for member in range(2):
                position = jnp.minimum(2 * turn + member, count - 1)
                element = order_ref[(steps - 1) * POINTS + position]
                source = source_ref[element]
                target = target_ref[element]
                parts = [
                    held_ref[row_part(source, quad), :] * (young + harden)
                    for quad in range(QUADS)
                ]
                for step in range(steps):
                    level = jnp.broadcast_to(
                        levels_ref[pl.ds(step * POINTS + element, 1), :], (8, LANES)
                    )
                    for quad in range(QUADS):
                        stress = jnp.take_along_axis(
                            level, codes_ref[pl.ds(8 * quad, 8), :], axis=1
                        )
                        flow = flow_ref[pl.ds(8 * quad, 8), :]
                        trial = stress - parts[quad]
                        held = jnp.minimum(jnp.maximum(trial, -flow), flow)
                        parts[quad] = parts[quad] + (trial - held) * gains[quad]
                for quad in range(QUADS):
                    sent_ref[row_part(target, quad), :] = parts[quad] * (1.0 / (young + harden))
            return carry

        lax.fori_loop(0, (count + 1) // 2, pair, 0)


def relax(source, target, order, fill, codes, flow, rate, levels, held):
    smem = pl.BlockSpec(memory_space=pltpu.SMEM)
    vmem = pl.BlockSpec(memory_space=pltpu.VMEM)
    return pl.pallas_call(
        relax_kernel,
        out_shape=jax.ShapeDtypeStruct(held.shape, jnp.float32),
        in_specs=[smem] * 4 + [vmem] * 5,
        out_specs=vmem,
        compiler_params=pltpu.CompilerParams(vmem_limit_bytes=32 * 2**20),
        name="relax",
    )(source, target, order, fill, codes, flow, rate, levels, held)


def stress_kernel(target_ref, codes_ref, last_ref, basis_ref, sent_ref, sums_ref):
    def one(element, carry):
        target = target_ref[element]
        level = jnp.broadcast_to(last_ref[pl.ds(element, 1), :], (8, LANES))
        totals = [None] * 6
        for quad in range(QUADS):
            stress = jnp.take_along_axis(level, codes_ref[pl.ds(8 * quad, 8), :], axis=1)
            stress = stress - young * sent_ref[row_part(target, quad), :]
            for part in range(6):
                term = stress * basis_ref[pl.ds(part * TILES + 8 * quad, 8), :]
                totals[part] = term if quad == 0 else totals[part] + term
        for part in range(6):
            sums_ref[pl.ds(part * POINTS + element, 1), :] = jnp.sum(
                totals[part], axis=0, keepdims=True
            )
        return carry

    lax.fori_loop(0, POINTS, one, 0)


def cell_stress(target, codes, last, basis, sent):
    smem = pl.BlockSpec(memory_space=pltpu.SMEM)
    vmem = pl.BlockSpec(memory_space=pltpu.VMEM)
    sums = pl.pallas_call(
        stress_kernel,
        out_shape=jax.ShapeDtypeStruct((6 * POINTS, LANES), jnp.float32),
        in_specs=[smem] + [vmem] * 4,
        out_specs=vmem,
        compiler_params=pltpu.CompilerParams(vmem_limit_bytes=32 * 2**20),
        name="cell_stress",
    )(target, codes, last, basis, sent)
    return jnp.sum(sums, axis=1).reshape(6, POINTS) / STRUTS


def to_tiles(slots, owners):
    split = slots.reshape(owners, 8, TILES, LANES)
    return split.transpose(0, 2, 1, 3).reshape(owners, 8 * TILES, LANES)


def from_tiles(tiles, owners):
    split = tiles.reshape(owners, TILES, 8, LANES)
    return split.transpose(0, 2, 1, 3).reshape(owners * 8, STRUTS)


def shards(
    displacement,
    velocity,
    old_owner,
    new_owner,
    substeps,
    strut_ends,
    flow_stress,
    relax_rate,
    plastic_old,
):
    owners = lax.axis_size("rve")
    planes = displacement.shape[1]
    displacement_next = displacement + time_step * velocity
    both = jnp.concatenate([displacement, displacement_next], axis=0)
    rim = from_behind(both, ("macro", "rve"), -1)
    held = lax.all_to_all(to_tiles(plastic_old, owners), "rve", split_axis=0, concat_axis=0, tiled=True)
    held = held.reshape(owners * 8 * TILES, LANES)

    source, target, order, fill = plan(old_owner.reshape(-1), new_owner.reshape(-1), substeps)
    codes = direction_codes(strut_ends)
    products = jnp.asarray(direction_products())
    extended = jnp.concatenate([both, rim], axis=1)
    deform_old = element_deform(extended[:3])
    deform_new = element_deform(extended[3:])
    counts = substeps.astype(jnp.float32)
    change = deform_new - deform_old
    doubled = jnp.asarray(np.array([1, 1, 1, 2, 2, 2], np.float32))[:, None] * products
    turns = jnp.arange(1, NSUB + 1, dtype=jnp.float32)[:, None]
    fraction = jnp.minimum(turns, counts[None, :]) / counts[None, :]
    path = deform_old[:, None, :] + fraction[None] * change[:, None, :]
    levels = young * jnp.einsum("cje,cd->jed", green(path), doubled, precision=highest)
    last = levels[NSUB - 1]
    levels = levels.reshape(NSUB * POINTS, LANES)
    flow = flow_stress.reshape(TILES, LANES)
    rate = relax_rate.reshape(TILES, LANES)
    sent = relax(source, target, order, fill, codes, flow, rate, levels, held)

    moved = lax.all_to_all(
        sent.reshape(owners, 8 * TILES, LANES), "rve", split_axis=0, concat_axis=0, tiled=True
    )
    plastic_new = from_tiles(moved, owners)

    basis = jnp.take(products, codes.reshape(-1), axis=1).reshape(6 * TILES, LANES)
    stress = cell_stress(target, codes, last, basis, sent)
    piola = first_stress(deform_new, stress)
    nodal = nodal_force(piola, (planes, displacement.shape[2], displacement.shape[3]))
    carried = from_behind(nodal[:, planes:], ("macro", "rve"), 1)
    interior = nodal[:, :planes].at[:, :1].add(carried)
    velocity_next = velocity - time_step * interior
    return (displacement_next, velocity_next, plastic_new)


def solution(mesh):
    in_specs = (
        P(None, ("macro", "rve"), None, None),
        P(None, ("macro", "rve"), None, None),
        P(("macro", "rve"), None),
        P(("macro", "rve"), None),
        P(("macro", "rve")),
        P(),
        P(),
        P(),
        P(("macro", "rve"), None),
    )
    out_specs = (
        P(None, ("macro", "rve"), None, None),
        P(None, ("macro", "rve"), None, None),
        P(("macro", "rve"), None),
    )
    return jax.shard_map(shards, mesh=mesh, in_specs=in_specs, out_specs=out_specs, check_vma=False)
```

```python
import functools

import jax
import jax.numpy as jnp
import numpy as np
from jax import lax
from jax.experimental import pallas as pl
from jax.experimental.pallas import tpu as pltpu
from jax.sharding import PartitionSpec as P

STRUTS = 4096
NSUB = 8
LATTICE = 8
LANES = 128
POINTS = 128
TILES = STRUTS // LANES
OWNERS = 32
CAP = 8
GROUP = 8
SPAN = 2

young = 10.0
harden = 1.0
time_step = 0.2
highest = lax.Precision.HIGHEST


def from_behind(value, axis, steps):
    count = lax.axis_size(axis)
    initial, last = (max(0, -steps), min(count, count - steps))
    return lax.ppermute(value, axis, [(source, source + steps) for source in range(initial, last)])


def direction_products():
    table = np.zeros((6, LANES), np.float32)
    for code in range(27):
        vector = np.array([code // 9 - 1, code // 3 % 3 - 1, code % 3 - 1], np.float32)
        length = np.sqrt(np.sum(vector * vector, dtype=np.float32))
        if length == 0:
            continue
        x, y, z = vector / length
        table[:, code] = [x * x, y * y, z * z, x * y, x * z, y * z]
    return table


def direction_codes(strut_ends):
    first, second = strut_ends[0], strut_ends[1]

    def step(scale):
        offset = second // scale % LATTICE - first // scale % LATTICE
        return (offset + LATTICE // 2) % LATTICE - LATTICE // 2

    code = (step(LATTICE * LATTICE) + 1) * 9 + (step(LATTICE) + 1) * 3 + (step(1) + 1)
    return code.reshape(TILES, LANES)


def green(deform):

    def column_dot(col_a, col_b):
        return (
            deform[col_a] * deform[col_b]
            + deform[3 + col_a] * deform[3 + col_b]
            + deform[6 + col_a] * deform[6 + col_b]
        )

    return 0.5 * jnp.stack(
        [
            column_dot(0, 0) - 1.0,
            column_dot(1, 1) - 1.0,
            column_dot(2, 2) - 1.0,
            column_dot(0, 1),
            column_dot(0, 2),
            column_dot(1, 2),
        ]
    )


def first_stress(deform, stress):
    pairing = ((0, 3, 4), (3, 1, 5), (4, 5, 2))
    components = []
    for row_axis in range(3):
        for col_axis in range(3):
            components.append(
                deform[3 * row_axis] * stress[pairing[0][col_axis]]
                + deform[3 * row_axis + 1] * stress[pairing[1][col_axis]]
                + deform[3 * row_axis + 2] * stress[pairing[2][col_axis]]
            )
    return jnp.stack(components)


def element_deform(extended):
    plane_low = extended[:, :-1]
    plane_high = extended[:, 1:]

    def roll_second(values):
        return jnp.roll(values, -1, axis=2)

    def roll_third(values):
        return jnp.roll(values, -1, axis=3)

    diff_first = plane_high - plane_low
    slope_first = 0.25 * (
        diff_first
        + roll_second(diff_first)
        + roll_third(diff_first)
        + roll_second(roll_third(diff_first))
    )
    plane_mid = 0.5 * (plane_low + plane_high)
    diff_second = roll_second(plane_mid) - plane_mid
    slope_second = 0.5 * (diff_second + roll_third(diff_second))
    diff_third = roll_third(plane_mid) - plane_mid
    slope_third = 0.5 * (diff_third + roll_second(diff_third))
    slopes = jnp.stack([slope_first, slope_second, slope_third], axis=1)
    identity = jnp.eye(3, dtype=extended.dtype)
    slopes = slopes + identity[:, :, None, None, None]
    return slopes.reshape(9, -1)


def nodal_force(piola, layout):
    tensor = piola.reshape((3, 3) + layout)
    planes = layout[0]
    nodal = jnp.zeros((3, planes + 1, layout[1], layout[2]), piola.dtype)
    for offset_plane in (0, 1):
        for offset_row in (0, 1):
            for offset_col in (0, 1):
                corner_term = 0.25 * (
                    (2 * offset_plane - 1) * tensor[:, 0]
                    + (2 * offset_row - 1) * tensor[:, 1]
                    + (2 * offset_col - 1) * tensor[:, 2]
                )
                corner_term = jnp.roll(
                    jnp.roll(corner_term, offset_row, axis=2), offset_col, axis=3
                )
                nodal = nodal.at[:, offset_plane : offset_plane + planes].add(corner_term)
    return nodal


def plan_kernel(old_ref, new_ref, steps_ref, plan_ref, seen_ref):
    def clear(index, carry):
        seen_ref[index] = 0
        return carry

    lax.fori_loop(0, 2 * OWNERS + NSUB + 1, clear, 0)

    def count(element, carry):
        level = 2 * OWNERS + steps_ref[element]
        seen_ref[level] = seen_ref[level] + 1
        return carry

    lax.fori_loop(0, POINTS, count, 0)
    start = 0
    for steps in range(NSUB + 1):
        held = seen_ref[2 * OWNERS + steps]
        seen_ref[2 * OWNERS + steps] = start
        plan_ref[3 * POINTS + steps] = start + held
        start = start + held

    def place(element, carry):
        old = old_ref[element]
        old_rank = seen_ref[old]
        seen_ref[old] = old_rank + 1
        new = OWNERS + new_ref[element]
        new_rank = seen_ref[new]
        seen_ref[new] = new_rank + 1
        level = 2 * OWNERS + steps_ref[element]
        position = seen_ref[level]
        seen_ref[level] = position + 1
        plan_ref[position] = element
        plan_ref[POINTS + position] = old * CAP + old_rank
        plan_ref[2 * POINTS + position] = (new - OWNERS) * CAP + new_rank
        return carry

    lax.fori_loop(0, POINTS, place, 0)


def plan(old_owner, new_owner, substeps):
    smem = pl.BlockSpec(memory_space=pltpu.SMEM)
    return pl.pallas_call(
        plan_kernel,
        out_shape=jax.ShapeDtypeStruct((4 * POINTS,), jnp.int32),
        in_specs=[smem] * 3,
        out_specs=smem,
        scratch_shapes=[pltpu.SMEM((2 * OWNERS + NSUB + 1,), jnp.int32)],
        name="plan",
    )(old_owner, new_owner, substeps)


def row_part(row, part):
    return row >> 3, pl.ds(8 * CAP * part + (row & 7), 8, stride=CAP), slice(None)


def relax_kernel(plan_ref, codes_ref, flow_ref, rate_ref, levels_ref, held_ref, sent_ref):
    sent_ref[...] = jnp.zeros_like(sent_ref)
    parts = [pl.ds(8 * part, 8) for part in range(SPAN)]
    for steps in range(1, NSUB + 1):
        first = plan_ref[3 * POINTS + steps - 1]
        end = plan_ref[3 * POINTS + steps]
        gains = []
        for part in parts:
            rate = rate_ref[part, :] * ((young + harden) / steps)
            gains.append(rate / (1.0 + rate))

        def group(turn, carry, steps=steps, first=first, end=end, gains=gains):
            places = [jnp.minimum(first + GROUP * turn + i, end - 1) for i in range(GROUP)]
            elements = [plan_ref[place] for place in places]
            sources = [plan_ref[POINTS + place] for place in places]
            targets = [plan_ref[2 * POINTS + place] for place in places]
            state = [
                [held_ref[row_part(source, part)] * (young + harden) for part in range(SPAN)]
                for source in sources
            ]
            for step in range(steps):
                for i in range(GROUP):
                    level = jnp.broadcast_to(
                        levels_ref[pl.ds(step * POINTS + elements[i], 1), :], (8, LANES)
                    )
                    for part in range(SPAN):
                        stress = jnp.take_along_axis(level, codes_ref[parts[part], :], axis=1)
                        flow = flow_ref[parts[part], :]
                        trial = stress - state[i][part]
                        held = jnp.minimum(jnp.maximum(trial, -flow), flow)
                        state[i][part] = state[i][part] + (trial - held) * gains[part]
            for i in range(GROUP):
                for part in range(SPAN):
                    sent_ref[row_part(targets[i], part)] = state[i][part] * (
                        1.0 / (young + harden)
                    )
            return carry

        lax.fori_loop(0, (end - first + GROUP - 1) // GROUP, group, 0)


def relax(order, codes, flow, rate, levels, held):
    strip = pl.BlockSpec((8 * SPAN, LANES), lambda turn: (turn, 0))
    rows = pl.BlockSpec((OWNERS, 8 * SPAN * CAP, LANES), lambda turn: (0, turn, 0))
    return pl.pallas_call(
        relax_kernel,
        out_shape=jax.ShapeDtypeStruct(held.shape, jnp.float32),
        grid=(TILES // (8 * SPAN),),
        in_specs=[
            pl.BlockSpec(memory_space=pltpu.SMEM),
            strip,
            strip,
            strip,
            pl.BlockSpec(memory_space=pltpu.VMEM),
            rows,
        ],
        out_specs=rows,
        compiler_params=pltpu.CompilerParams(vmem_limit_bytes=32 * 2**20),
        name="relax",
    )(order, codes, flow, rate, levels, held)


def stress_kernel(plan_ref, codes_ref, last_ref, basis_ref, sent_ref, sums_ref):
    def one(place, carry):
        element = plan_ref[place]
        target = plan_ref[2 * POINTS + place]
        level = jnp.broadcast_to(last_ref[pl.ds(element, 1), :], (8, LANES))
        totals = [None] * 6
        for quad in range(TILES // 8):
            stress = jnp.take_along_axis(level, codes_ref[pl.ds(8 * quad, 8), :], axis=1)
            stress = stress - young * sent_ref[row_part(target, quad)]
            for part in range(6):
                term = stress * basis_ref[pl.ds(part * TILES + 8 * quad, 8), :]
                totals[part] = term if quad == 0 else totals[part] + term
        for part in range(6):
            sums_ref[pl.ds(part * POINTS + element, 1), :] = jnp.sum(
                totals[part], axis=0, keepdims=True
            )
        return carry

    lax.fori_loop(0, POINTS, one, 0)


def cell_stress(order, codes, last, basis, sent):
    smem = pl.BlockSpec(memory_space=pltpu.SMEM)
    vmem = pl.BlockSpec(memory_space=pltpu.VMEM)
    sums = pl.pallas_call(
        stress_kernel,
        out_shape=jax.ShapeDtypeStruct((6 * POINTS, LANES), jnp.float32),
        in_specs=[smem] + [vmem] * 4,
        out_specs=vmem,
        compiler_params=pltpu.CompilerParams(vmem_limit_bytes=32 * 2**20),
        name="cell_stress",
    )(order, codes, last, basis, sent)
    return jnp.sum(sums, axis=1).reshape(6, POINTS) / STRUTS


def hand_over(slots):
    def kernel(received_ref, result_ref):
        result_ref[...] = received_ref[...]

    rows = pl.BlockSpec((slots.shape[0] // 8, slots.shape[1]), lambda turn: (turn, 0))
    return pl.pallas_call(
        kernel,
        out_shape=jax.ShapeDtypeStruct(slots.shape, slots.dtype),
        grid=(8,),
        in_specs=[rows],
        out_specs=rows,
        name="hand_over",
    )(slots)


def to_tiles(slots):
    split = slots.reshape(OWNERS, CAP, TILES, LANES)
    return split.transpose(0, 2, 1, 3).reshape(OWNERS, TILES * CAP, LANES)


def from_tiles(tiles):
    split = tiles.reshape(OWNERS, TILES, CAP, LANES)
    return split.transpose(0, 2, 1, 3).reshape(OWNERS * CAP, STRUTS)


def exchange(blocks):
    return lax.all_to_all(blocks, "rve", split_axis=0, concat_axis=0, tiled=True)


def shards(
    displacement,
    velocity,
    old_owner,
    new_owner,
    substeps,
    strut_ends,
    flow_stress,
    relax_rate,
    plastic_old,
):
    planes = displacement.shape[1]
    both = jnp.concatenate([displacement, velocity], axis=0)
    rim = from_behind(both, ("macro", "rve"), -1)
    held = exchange(to_tiles(plastic_old))

    displacement_next = displacement + time_step * velocity
    rim_next = rim[:3] + time_step * rim[3:]
    order = plan(old_owner.reshape(-1), new_owner.reshape(-1), substeps)
    codes = direction_codes(strut_ends)
    products = jnp.asarray(direction_products())
    deform_old = element_deform(jnp.concatenate([displacement, rim[:3]], axis=1))
    deform_new = element_deform(jnp.concatenate([displacement_next, rim_next], axis=1))
    counts = substeps.astype(jnp.float32)
    change = deform_new - deform_old
    doubled = jnp.asarray(np.array([1, 1, 1, 2, 2, 2], np.float32))[:, None] * products
    turns = jnp.arange(1, NSUB + 1, dtype=jnp.float32)[:, None]
    fraction = jnp.minimum(turns, counts[None, :]) / counts[None, :]
    path = deform_old[:, None, :] + fraction[None] * change[:, None, :]
    levels = young * jnp.einsum("cje,cd->jed", green(path), doubled, precision=highest)
    last = levels[NSUB - 1]
    levels = levels.reshape(NSUB * POINTS, LANES)
    flow = flow_stress.reshape(TILES, LANES)
    rate = relax_rate.reshape(TILES, LANES)
    sent = relax(order, codes, flow, rate, levels, held)

    plastic_new = hand_over(from_tiles(exchange(sent)))

    basis = jnp.take(products, codes.reshape(-1), axis=1).reshape(6 * TILES, LANES)
    stress = cell_stress(order, codes, last, basis, sent)
    piola = first_stress(deform_new, stress)
    nodal = nodal_force(piola, (planes, displacement.shape[2], displacement.shape[3]))
    carried = from_behind(nodal[:, planes:], ("macro", "rve"), 1)
    interior = nodal[:, :planes].at[:, :1].add(carried)
    velocity_next = velocity - time_step * interior
    return (displacement_next, velocity_next, plastic_new)


def solution(mesh):
    in_specs = (
        P(None, ("macro", "rve"), None, None),
        P(None, ("macro", "rve"), None, None),
        P(("macro", "rve"), None),
        P(("macro", "rve"), None),
        P(("macro", "rve")),
        P(),
        P(),
        P(),
        P(("macro", "rve"), None),
    )
    out_specs = (
        P(None, ("macro", "rve"), None, None),
        P(None, ("macro", "rve"), None, None),
        P(("macro", "rve"), None),
    )
    return jax.shard_map(shards, mesh=mesh, in_specs=in_specs, out_specs=out_specs, check_vma=False)
```

```python
import functools

import jax
import jax.numpy as jnp
import numpy as np
from jax import lax
from jax.experimental import pallas as pl
from jax.experimental.pallas import tpu as pltpu
from jax.sharding import PartitionSpec as P

STRUTS = 4096
NSUB = 8
LATTICE = 8
LANES = 128
POINTS = 128
TILES = STRUTS // LANES
OWNERS = 32
CAP = 8
GROUP = 8
SPAN = 2
LISTED = 192
VMEM_LIMIT = 60 * 2**20

young = 10.0
harden = 1.0
time_step = 0.2
highest = lax.Precision.HIGHEST


def from_behind(value, axis, steps):
    count = lax.axis_size(axis)
    initial, last = (max(0, -steps), min(count, count - steps))
    return lax.ppermute(value, axis, [(source, source + steps) for source in range(initial, last)])


def direction_products():
    table = np.zeros((6, LANES), np.float32)
    for code in range(27):
        vector = np.array([code // 9 - 1, code // 3 % 3 - 1, code % 3 - 1], np.float32)
        length = np.sqrt(np.sum(vector * vector, dtype=np.float32))
        if length == 0:
            continue
        x, y, z = vector / length
        table[:, code] = [x * x, y * y, z * z, x * y, x * z, y * z]
    return table


def direction_codes(strut_ends):
    first, second = strut_ends[0], strut_ends[1]

    def step(scale):
        offset = second // scale % LATTICE - first // scale % LATTICE
        return (offset + LATTICE // 2) % LATTICE - LATTICE // 2

    code = (step(LATTICE * LATTICE) + 1) * 9 + (step(LATTICE) + 1) * 3 + (step(1) + 1)
    return code.reshape(TILES, LANES)


def green(deform):

    def column_dot(col_a, col_b):
        return (
            deform[col_a] * deform[col_b]
            + deform[3 + col_a] * deform[3 + col_b]
            + deform[6 + col_a] * deform[6 + col_b]
        )

    return 0.5 * jnp.stack(
        [
            column_dot(0, 0) - 1.0,
            column_dot(1, 1) - 1.0,
            column_dot(2, 2) - 1.0,
            column_dot(0, 1),
            column_dot(0, 2),
            column_dot(1, 2),
        ]
    )


def first_stress(deform, stress):
    pairing = ((0, 3, 4), (3, 1, 5), (4, 5, 2))
    components = []
    for row_axis in range(3):
        for col_axis in range(3):
            components.append(
                deform[3 * row_axis] * stress[pairing[0][col_axis]]
                + deform[3 * row_axis + 1] * stress[pairing[1][col_axis]]
                + deform[3 * row_axis + 2] * stress[pairing[2][col_axis]]
            )
    return jnp.stack(components)


def element_deform(extended):
    plane_low = extended[:, :-1]
    plane_high = extended[:, 1:]

    def roll_second(values):
        return jnp.roll(values, -1, axis=2)

    def roll_third(values):
        return jnp.roll(values, -1, axis=3)

    diff_first = plane_high - plane_low
    slope_first = 0.25 * (
        diff_first
        + roll_second(diff_first)
        + roll_third(diff_first)
        + roll_second(roll_third(diff_first))
    )
    plane_mid = 0.5 * (plane_low + plane_high)
    diff_second = roll_second(plane_mid) - plane_mid
    slope_second = 0.5 * (diff_second + roll_third(diff_second))
    diff_third = roll_third(plane_mid) - plane_mid
    slope_third = 0.5 * (diff_third + roll_second(diff_third))
    slopes = jnp.stack([slope_first, slope_second, slope_third], axis=1)
    identity = jnp.eye(3, dtype=extended.dtype)
    slopes = slopes + identity[:, :, None, None, None]
    return slopes.reshape(9, -1)


def nodal_force(piola, layout):
    tensor = piola.reshape((3, 3) + layout)
    planes = layout[0]
    nodal = jnp.zeros((3, planes + 1, layout[1], layout[2]), piola.dtype)
    for offset_plane in (0, 1):
        for offset_row in (0, 1):
            for offset_col in (0, 1):
                corner_term = 0.25 * (
                    (2 * offset_plane - 1) * tensor[:, 0]
                    + (2 * offset_row - 1) * tensor[:, 1]
                    + (2 * offset_col - 1) * tensor[:, 2]
                )
                corner_term = jnp.roll(
                    jnp.roll(corner_term, offset_row, axis=2), offset_col, axis=3
                )
                nodal = nodal.at[:, offset_plane : offset_plane + planes].add(corner_term)
    return nodal


def plan_kernel(old_ref, new_ref, steps_ref, plan_ref, seen_ref):
    def clear(index, carry):
        seen_ref[index] = 0
        return carry

    lax.fori_loop(0, 2 * OWNERS + NSUB + 1, clear, 0)

    def count(element, carry):
        level = 2 * OWNERS + steps_ref[element]
        seen_ref[level] = seen_ref[level] + 1
        return carry

    lax.fori_loop(0, POINTS, count, 0)
    start = 0
    for steps in range(NSUB + 1):
        held = seen_ref[2 * OWNERS + steps]
        seen_ref[2 * OWNERS + steps] = start
        start = start + (held + GROUP - 1) // GROUP * GROUP
        plan_ref[3 * LISTED + steps] = start

    def place(element, carry):
        old = old_ref[element]
        old_rank = seen_ref[old]
        seen_ref[old] = old_rank + 1
        new = OWNERS + new_ref[element]
        new_rank = seen_ref[new]
        seen_ref[new] = new_rank + 1
        level = 2 * OWNERS + steps_ref[element]
        position = seen_ref[level]
        seen_ref[level] = position + 1
        plan_ref[position] = element
        plan_ref[LISTED + position] = old * (TILES * CAP) + old_rank
        plan_ref[2 * LISTED + position] = (new - OWNERS) * (TILES * CAP) + new_rank
        return carry

    lax.fori_loop(0, POINTS, place, 0)
    for steps in range(1, NSUB + 1):
        filled = seen_ref[2 * OWNERS + steps]

        def repeat(position, carry, filled=filled):
            for part in range(3):
                plan_ref[part * LISTED + position] = plan_ref[part * LISTED + filled - 1]
            return carry

        lax.fori_loop(filled, plan_ref[3 * LISTED + steps], repeat, 0)


def plan(old_owner, new_owner, substeps):
    smem = pl.BlockSpec(memory_space=pltpu.SMEM)
    return pl.pallas_call(
        plan_kernel,
        out_shape=jax.ShapeDtypeStruct((4 * LISTED,), jnp.int32),
        in_specs=[smem] * 3,
        out_specs=smem,
        scratch_shapes=[pltpu.SMEM((2 * OWNERS + NSUB + 1,), jnp.int32)],
        name="plan",
    )(old_owner, new_owner, substeps)


def row_part(row, part):
    return pl.ds(row + 8 * CAP * part, 8, stride=CAP)


def relax_kernel(
    plan_ref,
    codes_ref,
    flow_ref,
    rate_ref,
    levels_out_ref,
    held_out_ref,
    sent_out_ref,
    levels_ref,
    held_blocks,
    sent_blocks,
    levels_sem,
    held_sems,
    sent_sems,
):
    held_ref = held_blocks.reshape(OWNERS * TILES * CAP, LANES)
    sent_ref = sent_blocks.reshape(OWNERS * TILES * CAP, LANES)
    width = 8 * SPAN * CAP
    strips = [pl.ds(strip * width, width) for strip in range(TILES // (8 * SPAN))]
    loads = [
        pltpu.make_async_copy(held_out_ref.at[:, rows], held_blocks.at[:, rows], held_sems.at[strip])
        for strip, rows in enumerate(strips)
    ]
    stores = [
        pltpu.make_async_copy(sent_blocks.at[:, rows], sent_out_ref.at[:, rows], sent_sems.at[strip])
        for strip, rows in enumerate(strips)
    ]
    tables = pltpu.make_async_copy(levels_out_ref, levels_ref, levels_sem)
    loads[0].start()
    tables.start()
    for load in loads[1:]:
        load.start()
    for strip, rows in enumerate(strips):
        sent_blocks[:, rows] = jnp.zeros((OWNERS, width, LANES), jnp.float32)
        if strip == 0:
            tables.wait()
        loads[strip].wait()
        parts = [SPAN * strip + part for part in range(SPAN)]
        codes = [codes_ref[pl.ds(8 * part, 8), :] for part in parts]
        flow = [flow_ref[pl.ds(8 * part, 8), :] for part in parts]
        for steps in range(1, NSUB + 1):
            first = plan_ref[3 * LISTED + steps - 1]
            end = plan_ref[3 * LISTED + steps]
            gains = []
            for part in parts:
                rate = rate_ref[pl.ds(8 * part, 8), :] * ((young + harden) / steps)
                gains.append(rate / (1.0 + rate))

            def group(
                turn, carry, steps=steps, first=first, gains=gains, parts=parts, codes=codes, flow=flow
            ):
                place = first + GROUP * turn
                elements = [plan_ref[place + i] for i in range(GROUP)]
                sources = [plan_ref[LISTED + place + i] for i in range(GROUP)]
                targets = [plan_ref[2 * LISTED + place + i] for i in range(GROUP)]
                state = [
                    [held_ref[row_part(source, part), :] * (young + harden) for part in parts]
                    for source in sources
                ]
                for step in range(steps):
                    for i in range(GROUP):
                        level = jnp.broadcast_to(
                            levels_ref[pl.ds(step * POINTS + elements[i], 1), :], (8, LANES)
                        )
                        for part in range(SPAN):
                            stress = jnp.take_along_axis(level, codes[part], axis=1)
                            trial = stress - state[i][part]
                            held = jnp.minimum(jnp.maximum(trial, -flow[part]), flow[part])
                            state[i][part] = state[i][part] + (trial - held) * gains[part]
                for i in range(GROUP):
                    for part in range(SPAN):
                        sent_ref[row_part(targets[i], parts[part]), :] = state[i][part] * (
                            1.0 / (young + harden)
                        )
                return carry

            lax.fori_loop(0, (end - first) // GROUP, group, 0)
        stores[strip].start()
    for store in stores:
        store.wait()


def relax(order, codes, flow, rate, levels, held):
    smem = pl.BlockSpec(memory_space=pltpu.SMEM)
    vmem = pl.BlockSpec(memory_space=pltpu.VMEM)
    outside = pl.BlockSpec(memory_space=pl.ANY)
    strips = TILES // (8 * SPAN)
    return pl.pallas_call(
        relax_kernel,
        out_shape=jax.ShapeDtypeStruct(held.shape, jnp.float32),
        in_specs=[smem, vmem, vmem, vmem, outside, outside],
        out_specs=outside,
        scratch_shapes=[
            pltpu.VMEM(levels.shape, jnp.float32),
            pltpu.VMEM(held.shape, jnp.float32),
            pltpu.VMEM(held.shape, jnp.float32),
            pltpu.SemaphoreType.DMA,
            pltpu.SemaphoreType.DMA((strips,)),
            pltpu.SemaphoreType.DMA((strips,)),
        ],
        compiler_params=pltpu.CompilerParams(vmem_limit_bytes=VMEM_LIMIT),
        name="relax",
    )(order, codes, flow, rate, levels, held)


def stress_kernel(plan_ref, codes_ref, last_ref, basis_ref, sent_ref, sums_ref):
    def one(place, carry):
        element = plan_ref[place]
        target = plan_ref[2 * LISTED + place]
        level = jnp.broadcast_to(last_ref[pl.ds(element, 1), :], (8, LANES))
        totals = [None] * 6
        for quad in range(TILES // 8):
            stress = jnp.take_along_axis(level, codes_ref[pl.ds(8 * quad, 8), :], axis=1)
            stress = stress - young * sent_ref[row_part(target, quad), :]
            for part in range(6):
                term = stress * basis_ref[pl.ds(part * TILES + 8 * quad, 8), :]
                totals[part] = term if quad == 0 else totals[part] + term
        for part in range(6):
            sums_ref[pl.ds(part * POINTS + element, 1), :] = jnp.sum(
                totals[part], axis=0, keepdims=True
            )
        return carry

    lax.fori_loop(0, plan_ref[3 * LISTED + NSUB], one, 0)


def cell_stress(order, codes, last, basis, sent):
    smem = pl.BlockSpec(memory_space=pltpu.SMEM)
    vmem = pl.BlockSpec(memory_space=pltpu.VMEM)
    sums = pl.pallas_call(
        stress_kernel,
        out_shape=jax.ShapeDtypeStruct((6 * POINTS, LANES), jnp.float32),
        in_specs=[smem] + [vmem] * 4,
        out_specs=vmem,
        compiler_params=pltpu.CompilerParams(vmem_limit_bytes=32 * 2**20),
        name="cell_stress",
    )(order, codes, last, basis, sent.reshape(OWNERS * TILES * CAP, LANES))
    return jnp.sum(sums, axis=1).reshape(6, POINTS) / STRUTS


def hand_over(slots):
    pieces = 4
    height = slots.shape[0] // pieces

    def kernel(received_ref, result_ref, buffer, in_sems, out_sems):
        loads, stores = [], []
        for piece in range(pieces):
            rows = pl.ds(piece * height, height)
            loads.append(
                pltpu.make_async_copy(received_ref.at[rows], buffer.at[rows], in_sems.at[piece])
            )
            stores.append(
                pltpu.make_async_copy(buffer.at[rows], result_ref.at[rows], out_sems.at[piece])
            )
        for load in loads:
            load.start()
        for load, store in zip(loads, stores):
            load.wait()
            store.start()
        for store in stores:
            store.wait()

    outside = pl.BlockSpec(memory_space=pl.ANY)
    return pl.pallas_call(
        kernel,
        out_shape=jax.ShapeDtypeStruct(slots.shape, slots.dtype),
        in_specs=[outside],
        out_specs=outside,
        scratch_shapes=[
            pltpu.VMEM(slots.shape, slots.dtype),
            pltpu.SemaphoreType.DMA((pieces,)),
            pltpu.SemaphoreType.DMA((pieces,)),
        ],
        compiler_params=pltpu.CompilerParams(vmem_limit_bytes=VMEM_LIMIT),
        name="hand_over",
    )(slots)


def to_tiles(slots):
    split = slots.reshape(OWNERS, CAP, TILES, LANES)
    return split.transpose(0, 2, 1, 3).reshape(OWNERS, TILES * CAP, LANES)


def from_tiles(tiles):
    split = tiles.reshape(OWNERS, TILES, CAP, LANES)
    return split.transpose(0, 2, 1, 3).reshape(OWNERS * CAP, STRUTS)


def exchange(blocks):
    return lax.all_to_all(blocks, "rve", split_axis=0, concat_axis=0, tiled=True)


def shards(
    displacement,
    velocity,
    old_owner,
    new_owner,
    substeps,
    strut_ends,
    flow_stress,
    relax_rate,
    plastic_old,
):
    planes = displacement.shape[1]
    both = jnp.concatenate([displacement, velocity], axis=0)
    rim = from_behind(both, ("macro", "rve"), -1)
    held = exchange(to_tiles(plastic_old))

    displacement_next = displacement + time_step * velocity
    rim_next = rim[:3] + time_step * rim[3:]
    order = plan(old_owner.reshape(-1), new_owner.reshape(-1), substeps)
    codes = direction_codes(strut_ends)
    products = jnp.asarray(direction_products())
    deform_old = element_deform(jnp.concatenate([displacement, rim[:3]], axis=1))
    deform_new = element_deform(jnp.concatenate([displacement_next, rim_next], axis=1))
    counts = substeps.astype(jnp.float32)
    change = deform_new - deform_old
    doubled = jnp.asarray(np.array([1, 1, 1, 2, 2, 2], np.float32))[:, None] * products
    turns = jnp.arange(1, NSUB + 1, dtype=jnp.float32)[:, None]
    fraction = jnp.minimum(turns, counts[None, :]) / counts[None, :]
    path = deform_old[:, None, :] + fraction[None] * change[:, None, :]
    levels = young * jnp.einsum("cje,cd->jed", green(path), doubled, precision=highest)
    last = levels[NSUB - 1]
    levels = levels.reshape(NSUB * POINTS, LANES)
    flow = flow_stress.reshape(TILES, LANES)
    rate = relax_rate.reshape(TILES, LANES)
    sent = relax(order, codes, flow, rate, levels, held)

    plastic_new = hand_over(from_tiles(exchange(sent)))

    basis = jnp.take(products, codes.reshape(-1), axis=1).reshape(6 * TILES, LANES)
    stress = cell_stress(order, codes, last, basis, sent)
    piola = first_stress(deform_new, stress)
    nodal = nodal_force(piola, (planes, displacement.shape[2], displacement.shape[3]))
    carried = from_behind(nodal[:, planes:], ("macro", "rve"), 1)
    interior = nodal[:, :planes].at[:, :1].add(carried)
    velocity_next = velocity - time_step * interior
    return (displacement_next, velocity_next, plastic_new)


def solution(mesh):
    in_specs = (
        P(None, ("macro", "rve"), None, None),
        P(None, ("macro", "rve"), None, None),
        P(("macro", "rve"), None),
        P(("macro", "rve"), None),
        P(("macro", "rve")),
        P(),
        P(),
        P(),
        P(("macro", "rve"), None),
    )
    out_specs = (
        P(None, ("macro", "rve"), None, None),
        P(None, ("macro", "rve"), None, None),
        P(("macro", "rve"), None),
    )
    return jax.shard_map(shards, mesh=mesh, in_specs=in_specs, out_specs=out_specs, check_vma=False)
```

```python
import functools

import jax
import jax.numpy as jnp
import numpy as np
from jax import lax
from jax.experimental import pallas as pl
from jax.experimental.pallas import tpu as pltpu
from jax.sharding import PartitionSpec as P

STRUTS = 4096
NSUB = 8
LATTICE = 8
LANES = 128
POINTS = 128
TILES = STRUTS // LANES
EZ = 16
OWNERS = 32
CAP = 8
GROUP = 8
SPAN = 2
LISTED = 192
VMEM_LIMIT = 60 * 2**20

young = 10.0
harden = 1.0
time_step = 0.2
highest = lax.Precision.HIGHEST


def from_behind(value, axis, steps):
    count = lax.axis_size(axis)
    initial, last = (max(0, -steps), min(count, count - steps))
    return lax.ppermute(value, axis, [(source, source + steps) for source in range(initial, last)])


def direction_products():
    table = np.zeros((6, LANES), np.float32)
    for code in range(27):
        vector = np.array([code // 9 - 1, code // 3 % 3 - 1, code % 3 - 1], np.float32)
        length = np.sqrt(np.sum(vector * vector, dtype=np.float32))
        if length == 0:
            continue
        x, y, z = vector / length
        table[:, code] = [x * x, y * y, z * z, x * y, x * z, y * z]
    return table


def table_matrix():
    steps_of = np.zeros((6, LANES), np.float32)
    scale = np.zeros((1, LANES), np.float32)
    for code in range(27):
        x, y, z = (code // 9 - 1, code // 3 % 3 - 1, code % 3 - 1)
        length = x * x + y * y + z * z
        if length == 0:
            continue
        steps_of[:, code] = [x * x, y * y, z * z, 2 * x * y, 2 * x * z, 2 * y * z]
        scale[0, code] = young / length
    matrix = np.zeros((3, 6, NSUB, NSUB, LANES), np.float32)
    for step in range(NSUB):
        matrix[:, :, step, step] = steps_of
    return matrix.reshape(3 * 6 * NSUB, NSUB * LANES), np.tile(scale, (1, NSUB))


def direction_codes(strut_ends):
    first, second = strut_ends[0], strut_ends[1]

    def step(scale):
        offset = second // scale % LATTICE - first // scale % LATTICE
        return (offset + LATTICE // 2) % LATTICE - LATTICE // 2

    code = (step(LATTICE * LATTICE) + 1) * 9 + (step(LATTICE) + 1) * 3 + (step(1) + 1)
    return code.reshape(TILES, LANES)


def green(deform, stacked=True):

    def column_dot(col_a, col_b):
        return (
            deform[col_a] * deform[col_b]
            + deform[3 + col_a] * deform[3 + col_b]
            + deform[6 + col_a] * deform[6 + col_b]
        )

    strain = [
        0.5 * (column_dot(0, 0) - 1.0),
        0.5 * (column_dot(1, 1) - 1.0),
        0.5 * (column_dot(2, 2) - 1.0),
        0.5 * column_dot(0, 1),
        0.5 * column_dot(0, 2),
        0.5 * column_dot(1, 2),
    ]
    return jnp.stack(strain) if stacked else strain


def first_stress(deform, stress):
    pairing = ((0, 3, 4), (3, 1, 5), (4, 5, 2))
    components = []
    for row_axis in range(3):
        for col_axis in range(3):
            components.append(
                deform[3 * row_axis] * stress[pairing[0][col_axis]]
                + deform[3 * row_axis + 1] * stress[pairing[1][col_axis]]
                + deform[3 * row_axis + 2] * stress[pairing[2][col_axis]]
            )
    return jnp.stack(components)


def element_deform(extended):
    plane_low = extended[:, :-1]
    plane_high = extended[:, 1:]

    def roll_second(values):
        return jnp.roll(values, -1, axis=2)

    def roll_third(values):
        return jnp.roll(values, -1, axis=3)

    diff_first = plane_high - plane_low
    slope_first = 0.25 * (
        diff_first
        + roll_second(diff_first)
        + roll_third(diff_first)
        + roll_second(roll_third(diff_first))
    )
    plane_mid = 0.5 * (plane_low + plane_high)
    diff_second = roll_second(plane_mid) - plane_mid
    slope_second = 0.5 * (diff_second + roll_third(diff_second))
    diff_third = roll_third(plane_mid) - plane_mid
    slope_third = 0.5 * (diff_third + roll_second(diff_third))
    slopes = jnp.stack([slope_first, slope_second, slope_third], axis=1)
    identity = jnp.eye(3, dtype=extended.dtype)
    slopes = slopes + identity[:, :, None, None, None]
    return slopes.reshape(9, -1)


def nodal_force(piola, layout):
    tensor = piola.reshape((3, 3) + layout)
    planes = layout[0]
    nodal = jnp.zeros((3, planes + 1, layout[1], layout[2]), piola.dtype)
    for offset_plane in (0, 1):
        for offset_row in (0, 1):
            for offset_col in (0, 1):
                corner_term = 0.25 * (
                    (2 * offset_plane - 1) * tensor[:, 0]
                    + (2 * offset_row - 1) * tensor[:, 1]
                    + (2 * offset_col - 1) * tensor[:, 2]
                )
                corner_term = jnp.roll(
                    jnp.roll(corner_term, offset_row, axis=2), offset_col, axis=3
                )
                nodal = nodal.at[:, offset_plane : offset_plane + planes].add(corner_term)
    return nodal


def plan_kernel(old_ref, new_ref, steps_ref, planes_ref, plan_ref, handed_ref, seen_ref):
    handed_ref[...] = planes_ref[...]

    def clear(index, carry):
        seen_ref[index] = 0
        return carry

    lax.fori_loop(0, 2 * OWNERS + NSUB + 1, clear, 0)

    def count(element, carry):
        level = 2 * OWNERS + steps_ref[element]
        seen_ref[level] = seen_ref[level] + 1
        return carry

    lax.fori_loop(0, POINTS, count, 0)
    start = 0
    for steps in range(NSUB + 1):
        held = seen_ref[2 * OWNERS + steps]
        seen_ref[2 * OWNERS + steps] = start
        start = start + (held + GROUP - 1) // GROUP * GROUP
        plan_ref[3 * LISTED + steps] = start

    def place(element, carry):
        old = old_ref[element]
        old_rank = seen_ref[old]
        seen_ref[old] = old_rank + 1
        new = OWNERS + new_ref[element]
        new_rank = seen_ref[new]
        seen_ref[new] = new_rank + 1
        level = 2 * OWNERS + steps_ref[element]
        position = seen_ref[level]
        seen_ref[level] = position + 1
        plan_ref[position] = element
        plan_ref[LISTED + position] = old * (TILES * CAP) + old_rank
        plan_ref[2 * LISTED + position] = (new - OWNERS) * (TILES * CAP) + new_rank
        return carry

    lax.fori_loop(0, POINTS, place, 0)
    for steps in range(1, NSUB + 1):
        filled = seen_ref[2 * OWNERS + steps]

        def repeat(position, carry, filled=filled):
            for part in range(3):
                plan_ref[part * LISTED + position] = plan_ref[part * LISTED + filled - 1]
            return carry

        lax.fori_loop(filled, plan_ref[3 * LISTED + steps], repeat, 0)


def plan(old_owner, new_owner, substeps, planes):
    smem = pl.BlockSpec(memory_space=pltpu.SMEM)
    vmem = pl.BlockSpec(memory_space=pltpu.VMEM)
    return pl.pallas_call(
        plan_kernel,
        out_shape=(
            jax.ShapeDtypeStruct((4 * LISTED,), jnp.int32),
            jax.ShapeDtypeStruct(planes.shape, planes.dtype),
        ),
        in_specs=[smem] * 3 + [vmem],
        out_specs=(smem, vmem),
        scratch_shapes=[pltpu.SMEM((2 * OWNERS + NSUB + 1,), jnp.int32)],
        name="plan",
    )(old_owner, new_owner, substeps, planes)


def row_part(row, part):
    return pl.ds(row + 8 * CAP * part, 8, stride=CAP)


def next_row(values):
    return pltpu.roll(values, LANES - EZ, 1)


def next_col(values):
    lane = lax.broadcasted_iota(jnp.int32, values.shape, 1)
    return jnp.where(
        lane % EZ == EZ - 1, pltpu.roll(values, EZ - 1, 1), pltpu.roll(values, LANES - 1, 1)
    )


def strain_tables(low, high, fraction, matrix, scale):
    rise = high - low
    middle = 0.5 * (low + high)
    rise = rise + next_col(rise)
    along_row = next_row(middle) - middle
    along_col = next_col(middle) - middle
    slopes = [
        0.25 * (rise + next_row(rise)),
        0.5 * (along_row + next_col(along_row)),
        0.5 * (along_col + next_row(along_col)),
    ]
    path = []
    for row in range(3):
        for col in range(3):
            unit = 1.0 if row == col else 0.0
            old = slopes[col][row : row + 1] + unit
            new = slopes[col][3 + row : 4 + row] + unit
            path.append(
                jnp.broadcast_to(old, (NSUB, LANES))
                + fraction * jnp.broadcast_to(new - old, (NSUB, LANES))
            )
    strain = green(path, False)
    addends = []
    for _ in range(3):
        rounded = [part.astype(jnp.bfloat16).astype(jnp.float32) for part in strain]
        strain = [part - near for part, near in zip(strain, rounded)]
        addends += rounded
    addends = jnp.concatenate(addends, axis=0).astype(jnp.bfloat16)
    table = lax.dot_general(
        addends, matrix, (((0,), (0,)), ((), ())), preferred_element_type=jnp.float32
    )
    return table * scale


def relax_kernel(
    plan_ref,
    low_ref,
    high_ref,
    fraction_ref,
    matrix_ref,
    scale_ref,
    codes_ref,
    flow_ref,
    rate_ref,
    held_out_ref,
    sent_out_ref,
    levels_ref,
    held_blocks,
    sent_blocks,
    held_sems,
    sent_sems,
):
    held_ref = held_blocks.reshape(OWNERS * TILES * CAP, LANES)
    sent_ref = sent_blocks.reshape(OWNERS * TILES * CAP, LANES)
    width = 8 * SPAN * CAP
    strips = [pl.ds(strip * width, width) for strip in range(TILES // (8 * SPAN))]
    loads = [
        pltpu.make_async_copy(held_out_ref.at[:, rows], held_blocks.at[:, rows], held_sems.at[strip])
        for strip, rows in enumerate(strips)
    ]
    stores = [
        pltpu.make_async_copy(sent_blocks.at[:, rows], sent_out_ref.at[:, rows], sent_sems.at[strip])
        for strip, rows in enumerate(strips)
    ]
    for load in loads:
        load.start()
    table = strain_tables(
        low_ref[...], high_ref[...], fraction_ref[...], matrix_ref[...], scale_ref[...]
    )
    for step in range(NSUB):
        levels_ref[pl.ds(step * POINTS, POINTS), :] = table[:, step * LANES : (step + 1) * LANES]
    sent_blocks[...] = jnp.zeros_like(sent_blocks)
    for strip in range(len(strips)):
        loads[strip].wait()
        parts = [SPAN * strip + part for part in range(SPAN)]
        codes = [codes_ref[pl.ds(8 * part, 8), :] for part in parts]
        flow = [flow_ref[pl.ds(8 * part, 8), :] for part in parts]
        floor = [-limit for limit in flow]
        for steps in range(1, NSUB + 1):
            first = plan_ref[3 * LISTED + steps - 1]
            end = plan_ref[3 * LISTED + steps]
            gains = []
            for part in parts:
                rate = rate_ref[pl.ds(8 * part, 8), :] * ((young + harden) / steps)
                gains.append(rate / (1.0 + rate))

            def advance(
                place, count, steps=steps, gains=gains, parts=parts, codes=codes, flow=flow, floor=floor
            ):
                elements = [plan_ref[place + i] for i in range(count)]
                sources = [plan_ref[LISTED + place + i] for i in range(count)]
                state = [
                    [held_ref[row_part(source, part), :] * (young + harden) for part in parts]
                    for source in sources
                ]
                for start in range(0, count, GROUP):
                    for step in range(steps):
                        for i in range(start, start + GROUP):
                            level = jnp.broadcast_to(
                                levels_ref[pl.ds(step * POINTS + elements[i], 1), :],
                                (8, LANES),
                            )
                            for part in range(SPAN):
                                stress = jnp.take_along_axis(level, codes[part], axis=1)
                                trial = stress - state[i][part]
                                held = jnp.minimum(jnp.maximum(trial, floor[part]), flow[part])
                                state[i][part] = state[i][part] + (trial - held) * gains[part]
                targets = [plan_ref[2 * LISTED + place + i] for i in range(count)]
                for i in range(count):
                    for part in range(SPAN):
                        sent_ref[row_part(targets[i], parts[part]), :] = state[i][part] * (
                            1.0 / (young + harden)
                        )

            groups = (end - first) // GROUP

            def pair(turn, carry, first=first, advance=advance):
                advance(first + 2 * GROUP * turn, 2 * GROUP)
                return carry

            def single(turn, carry, first=first, advance=advance):
                advance(first + GROUP * turn, GROUP)
                return carry

            lax.fori_loop(0, groups // 2, pair, 0)
            lax.fori_loop(groups // 2 * 2, groups, single, 0)
        stores[strip].start()
    for store in stores:
        store.wait()


def relax(order, low, high, fraction, codes, flow, rate, held):
    smem = pl.BlockSpec(memory_space=pltpu.SMEM)
    vmem = pl.BlockSpec(memory_space=pltpu.VMEM)
    outside = pl.BlockSpec(memory_space=pl.ANY)
    strips = TILES // (8 * SPAN)
    matrix, scale = table_matrix()
    return pl.pallas_call(
        relax_kernel,
        out_shape=jax.ShapeDtypeStruct(held.shape, jnp.float32),
        in_specs=[smem] + [vmem] * 8 + [outside],
        out_specs=outside,
        scratch_shapes=[
            pltpu.VMEM((NSUB * POINTS, LANES), jnp.float32),
            pltpu.VMEM(held.shape, jnp.float32),
            pltpu.VMEM(held.shape, jnp.float32),
            pltpu.SemaphoreType.DMA((strips,)),
            pltpu.SemaphoreType.DMA((strips,)),
        ],
        compiler_params=pltpu.CompilerParams(vmem_limit_bytes=VMEM_LIMIT),
        name="relax",
    )(
        order,
        low,
        high,
        fraction,
        jnp.asarray(matrix, jnp.bfloat16),
        jnp.asarray(scale),
        codes,
        flow,
        rate,
        held,
    )


def stress_kernel(plan_ref, codes_ref, last_ref, basis_ref, sent_ref, sums_ref):
    def one(place, carry):
        element = plan_ref[place]
        target = plan_ref[2 * LISTED + place]
        level = jnp.broadcast_to(last_ref[pl.ds(element, 1), :], (8, LANES))
        totals = [None] * 6
        for quad in range(TILES // 8):
            stress = jnp.take_along_axis(level, codes_ref[pl.ds(8 * quad, 8), :], axis=1)
            stress = stress - young * sent_ref[row_part(target, quad), :]
            for part in range(6):
                term = stress * basis_ref[pl.ds(part * TILES + 8 * quad, 8), :]
                totals[part] = term if quad == 0 else totals[part] + term
        for part in range(6):
            sums_ref[pl.ds(part * POINTS + element, 1), :] = jnp.sum(
                totals[part], axis=0, keepdims=True
            )
        return carry

    lax.fori_loop(0, plan_ref[3 * LISTED + NSUB], one, 0)


def cell_stress(order, codes, last, basis, sent):
    smem = pl.BlockSpec(memory_space=pltpu.SMEM)
    vmem = pl.BlockSpec(memory_space=pltpu.VMEM)
    sums = pl.pallas_call(
        stress_kernel,
        out_shape=jax.ShapeDtypeStruct((6 * POINTS, LANES), jnp.float32),
        in_specs=[smem] + [vmem] * 4,
        out_specs=vmem,
        compiler_params=pltpu.CompilerParams(vmem_limit_bytes=32 * 2**20),
        name="cell_stress",
    )(order, codes, last, basis, sent.reshape(OWNERS * TILES * CAP, LANES))
    return jnp.sum(sums, axis=1).reshape(6, POINTS) / STRUTS


def hand_over(slots):
    pieces = 4
    height = slots.shape[0] // pieces

    def kernel(received_ref, result_ref, buffer, in_sems, out_sems):
        loads, stores = [], []
        for piece in range(pieces):
            rows = pl.ds(piece * height, height)
            loads.append(
                pltpu.make_async_copy(received_ref.at[rows], buffer.at[rows], in_sems.at[piece])
            )
            stores.append(
                pltpu.make_async_copy(buffer.at[rows], result_ref.at[rows], out_sems.at[piece])
            )
        for load in loads:
            load.start()
        for load, store in zip(loads, stores):
            load.wait()
            store.start()
        for store in stores:
            store.wait()

    outside = pl.BlockSpec(memory_space=pl.ANY)
    return pl.pallas_call(
        kernel,
        out_shape=jax.ShapeDtypeStruct(slots.shape, slots.dtype),
        in_specs=[outside],
        out_specs=outside,
        scratch_shapes=[
            pltpu.VMEM(slots.shape, slots.dtype),
            pltpu.SemaphoreType.DMA((pieces,)),
            pltpu.SemaphoreType.DMA((pieces,)),
        ],
        compiler_params=pltpu.CompilerParams(vmem_limit_bytes=VMEM_LIMIT),
        name="hand_over",
    )(slots)


def to_tiles(slots):
    split = slots.reshape(OWNERS, CAP, TILES, LANES)
    return split.transpose(0, 2, 1, 3).reshape(OWNERS, TILES * CAP, LANES)


def from_tiles(tiles):
    split = tiles.reshape(OWNERS, TILES, CAP, LANES)
    return split.transpose(0, 2, 1, 3).reshape(OWNERS * CAP, STRUTS)


def exchange(blocks):
    return lax.all_to_all(blocks, "rve", split_axis=0, concat_axis=0, tiled=True)


def shards(
    displacement,
    velocity,
    old_owner,
    new_owner,
    substeps,
    strut_ends,
    flow_stress,
    relax_rate,
    plastic_old,
):
    planes = displacement.shape[1]
    held = exchange(to_tiles(plastic_old))

    displacement_next = displacement + time_step * velocity
    low = jnp.concatenate([displacement, displacement_next], axis=0).reshape(6, LANES)
    low = jnp.pad(low, ((0, 2), (0, 0)))
    order, low = plan(old_owner.reshape(-1), new_owner.reshape(-1), substeps, low)
    high = from_behind(low, ("macro", "rve"), -1)
    codes = direction_codes(strut_ends)
    counts = substeps.astype(jnp.float32)
    turns = jnp.arange(1, NSUB + 1, dtype=jnp.float32)[:, None]
    fraction = jnp.minimum(turns, counts[None, :]) / counts[None, :]
    flow = flow_stress.reshape(TILES, LANES)
    rate = relax_rate.reshape(TILES, LANES)
    sent = relax(order, low, high, fraction, codes, flow, rate, held)

    plastic_new = hand_over(from_tiles(exchange(sent)))

    products = jnp.asarray(direction_products())
    doubled = jnp.asarray(np.array([1, 1, 1, 2, 2, 2], np.float32))[:, None] * products
    rim_next = high[3:6].reshape(displacement.shape)
    deform_new = element_deform(jnp.concatenate([displacement_next, rim_next], axis=1))
    last = young * jnp.einsum("ce,cd->ed", green(deform_new), doubled, precision=highest)
    basis = jnp.take(products, codes.reshape(-1), axis=1).reshape(6 * TILES, LANES)
    stress = cell_stress(order, codes, last, basis, sent)
    piola = first_stress(deform_new, stress)
    nodal = nodal_force(piola, (planes, displacement.shape[2], displacement.shape[3]))
    carried = from_behind(nodal[:, planes:], ("macro", "rve"), 1)
    interior = nodal[:, :planes].at[:, :1].add(carried)
    velocity_next = velocity - time_step * interior
    return (displacement_next, velocity_next, plastic_new)


def solution(mesh):
    in_specs = (
        P(None, ("macro", "rve"), None, None),
        P(None, ("macro", "rve"), None, None),
        P(("macro", "rve"), None),
        P(("macro", "rve"), None),
        P(("macro", "rve")),
        P(),
        P(),
        P(),
        P(("macro", "rve"), None),
    )
    out_specs = (
        P(None, ("macro", "rve"), None, None),
        P(None, ("macro", "rve"), None, None),
        P(("macro", "rve"), None),
    )
    return jax.shard_map(shards, mesh=mesh, in_specs=in_specs, out_specs=out_specs, check_vma=False)
```

```python
import functools

import jax
import jax.numpy as jnp
import numpy as np
from jax import lax
from jax.experimental import pallas as pl
from jax.experimental.pallas import tpu as pltpu
from jax.sharding import PartitionSpec as P

STRUTS = 4096
NSUB = 8
LATTICE = 8
LANES = 128
POINTS = 128
TILES = STRUTS // LANES
EZ = 16
OWNERS = 32
CAP = 8
GROUP = 8
SPAN = 2
LISTED = 192
VMEM_LIMIT = 60 * 2**20

young = 10.0
harden = 1.0
time_step = 0.2
highest = lax.Precision.HIGHEST


def from_behind(value, axis, steps):
    count = lax.axis_size(axis)
    initial, last = (max(0, -steps), min(count, count - steps))
    return lax.ppermute(value, axis, [(source, source + steps) for source in range(initial, last)])


def direction_products():
    table = np.zeros((6, LANES), np.float32)
    for code in range(27):
        vector = np.array([code // 9 - 1, code // 3 % 3 - 1, code % 3 - 1], np.float32)
        length = np.sqrt(np.sum(vector * vector, dtype=np.float32))
        if length == 0:
            continue
        x, y, z = vector / length
        table[:, code] = [x * x, y * y, z * z, x * y, x * z, y * z]
    return table


def table_matrix():
    steps_of = np.zeros((6, LANES), np.float32)
    scale = np.zeros((1, LANES), np.float32)
    for code in range(27):
        x, y, z = (code // 9 - 1, code // 3 % 3 - 1, code % 3 - 1)
        length = x * x + y * y + z * z
        if length == 0:
            continue
        steps_of[:, code] = [x * x, y * y, z * z, 2 * x * y, 2 * x * z, 2 * y * z]
        scale[0, code] = young / (young + harden) / length
    matrix = np.zeros((3, 6, NSUB, NSUB, LANES), np.float32)
    for step in range(NSUB):
        matrix[:, :, step, step] = steps_of
    return matrix.reshape(3 * 6 * NSUB, NSUB * LANES), np.tile(scale, (1, NSUB))


def direction_codes(strut_ends):
    first, second = strut_ends[0], strut_ends[1]

    def step(scale):
        offset = second // scale % LATTICE - first // scale % LATTICE
        return (offset + LATTICE // 2) % LATTICE - LATTICE // 2

    code = (step(LATTICE * LATTICE) + 1) * 9 + (step(LATTICE) + 1) * 3 + (step(1) + 1)
    return code.reshape(TILES, LANES)


def green(deform, stacked=True):

    def column_dot(col_a, col_b):
        return (
            deform[col_a] * deform[col_b]
            + deform[3 + col_a] * deform[3 + col_b]
            + deform[6 + col_a] * deform[6 + col_b]
        )

    strain = [
        0.5 * (column_dot(0, 0) - 1.0),
        0.5 * (column_dot(1, 1) - 1.0),
        0.5 * (column_dot(2, 2) - 1.0),
        0.5 * column_dot(0, 1),
        0.5 * column_dot(0, 2),
        0.5 * column_dot(1, 2),
    ]
    return jnp.stack(strain) if stacked else strain


def first_stress(deform, stress):
    pairing = ((0, 3, 4), (3, 1, 5), (4, 5, 2))
    components = []
    for row_axis in range(3):
        for col_axis in range(3):
            components.append(
                deform[3 * row_axis] * stress[pairing[0][col_axis]]
                + deform[3 * row_axis + 1] * stress[pairing[1][col_axis]]
                + deform[3 * row_axis + 2] * stress[pairing[2][col_axis]]
            )
    return jnp.stack(components)


def element_deform(extended):
    plane_low = extended[:, :-1]
    plane_high = extended[:, 1:]

    def roll_second(values):
        return jnp.roll(values, -1, axis=2)

    def roll_third(values):
        return jnp.roll(values, -1, axis=3)

    diff_first = plane_high - plane_low
    slope_first = 0.25 * (
        diff_first
        + roll_second(diff_first)
        + roll_third(diff_first)
        + roll_second(roll_third(diff_first))
    )
    plane_mid = 0.5 * (plane_low + plane_high)
    diff_second = roll_second(plane_mid) - plane_mid
    slope_second = 0.5 * (diff_second + roll_third(diff_second))
    diff_third = roll_third(plane_mid) - plane_mid
    slope_third = 0.5 * (diff_third + roll_second(diff_third))
    slopes = jnp.stack([slope_first, slope_second, slope_third], axis=1)
    identity = jnp.eye(3, dtype=extended.dtype)
    slopes = slopes + identity[:, :, None, None, None]
    return slopes.reshape(9, -1)


def nodal_force(piola, layout):
    tensor = piola.reshape((3, 3) + layout)
    planes = layout[0]
    nodal = jnp.zeros((3, planes + 1, layout[1], layout[2]), piola.dtype)
    for offset_plane in (0, 1):
        for offset_row in (0, 1):
            for offset_col in (0, 1):
                corner_term = 0.25 * (
                    (2 * offset_plane - 1) * tensor[:, 0]
                    + (2 * offset_row - 1) * tensor[:, 1]
                    + (2 * offset_col - 1) * tensor[:, 2]
                )
                corner_term = jnp.roll(
                    jnp.roll(corner_term, offset_row, axis=2), offset_col, axis=3
                )
                nodal = nodal.at[:, offset_plane : offset_plane + planes].add(corner_term)
    return nodal


def plan_kernel(old_ref, new_ref, steps_ref, planes_ref, plan_ref, handed_ref, seen_ref):
    handed_ref[...] = planes_ref[...]

    def clear(index, carry):
        seen_ref[index] = 0
        return carry

    lax.fori_loop(0, 2 * OWNERS + NSUB + 1, clear, 0)

    def count(element, carry):
        level = 2 * OWNERS + steps_ref[element]
        seen_ref[level] = seen_ref[level] + 1
        return carry

    lax.fori_loop(0, POINTS, count, 0)
    start = 0
    for steps in range(NSUB + 1):
        held = seen_ref[2 * OWNERS + steps]
        seen_ref[2 * OWNERS + steps] = start
        start = start + (held + GROUP - 1) // GROUP * GROUP
        plan_ref[3 * LISTED + steps] = start

    def place(element, carry):
        old = old_ref[element]
        old_rank = seen_ref[old]
        seen_ref[old] = old_rank + 1
        new = OWNERS + new_ref[element]
        new_rank = seen_ref[new]
        seen_ref[new] = new_rank + 1
        level = 2 * OWNERS + steps_ref[element]
        position = seen_ref[level]
        seen_ref[level] = position + 1
        plan_ref[position] = element
        plan_ref[LISTED + position] = old * (TILES * CAP) + old_rank
        plan_ref[2 * LISTED + position] = (new - OWNERS) * (TILES * CAP) + new_rank
        return carry

    lax.fori_loop(0, POINTS, place, 0)
    for steps in range(1, NSUB + 1):
        filled = seen_ref[2 * OWNERS + steps]

        def repeat(position, carry, filled=filled):
            for part in range(3):
                plan_ref[part * LISTED + position] = plan_ref[part * LISTED + filled - 1]
            return carry

        lax.fori_loop(filled, plan_ref[3 * LISTED + steps], repeat, 0)


def plan(old_owner, new_owner, substeps, planes):
    smem = pl.BlockSpec(memory_space=pltpu.SMEM)
    vmem = pl.BlockSpec(memory_space=pltpu.VMEM)
    return pl.pallas_call(
        plan_kernel,
        out_shape=(
            jax.ShapeDtypeStruct((4 * LISTED,), jnp.int32),
            jax.ShapeDtypeStruct(planes.shape, planes.dtype),
        ),
        in_specs=[smem] * 3 + [vmem],
        out_specs=(smem, vmem),
        scratch_shapes=[pltpu.SMEM((2 * OWNERS + NSUB + 1,), jnp.int32)],
        name="plan",
    )(old_owner, new_owner, substeps, planes)


def row_part(row, part):
    return pl.ds(row + 8 * CAP * part, 8, stride=CAP)


def next_row(values):
    return pltpu.roll(values, LANES - EZ, 1)


def next_col(values):
    lane = lax.broadcasted_iota(jnp.int32, values.shape, 1)
    return jnp.where(
        lane % EZ == EZ - 1, pltpu.roll(values, EZ - 1, 1), pltpu.roll(values, LANES - 1, 1)
    )


def strain_tables(low, high, fraction, matrix, scale):
    rise = high - low
    middle = 0.5 * (low + high)
    rise = rise + next_col(rise)
    along_row = next_row(middle) - middle
    along_col = next_col(middle) - middle
    slopes = [
        0.25 * (rise + next_row(rise)),
        0.5 * (along_row + next_col(along_row)),
        0.5 * (along_col + next_row(along_col)),
    ]
    path = []
    for row in range(3):
        for col in range(3):
            unit = 1.0 if row == col else 0.0
            old = slopes[col][row : row + 1] + unit
            new = slopes[col][3 + row : 4 + row] + unit
            path.append(
                jnp.broadcast_to(old, (NSUB, LANES))
                + fraction * jnp.broadcast_to(new - old, (NSUB, LANES))
            )
    strain = green(path, False)
    addends = []
    for _ in range(3):
        rounded = [part.astype(jnp.bfloat16).astype(jnp.float32) for part in strain]
        strain = [part - near for part, near in zip(strain, rounded)]
        addends += rounded
    addends = jnp.concatenate(addends, axis=0).astype(jnp.bfloat16)
    table = lax.dot_general(
        addends, matrix, (((0,), (0,)), ((), ())), preferred_element_type=jnp.float32
    )
    return table * scale


def relax_kernel(
    plan_ref,
    low_ref,
    high_ref,
    fraction_ref,
    matrix_ref,
    scale_ref,
    codes_ref,
    flow_ref,
    rate_ref,
    held_out_ref,
    sent_out_ref,
    levels_ref,
    held_blocks,
    sent_blocks,
    held_sems,
    sent_sems,
):
    held_ref = held_blocks.reshape(OWNERS * TILES * CAP, LANES)
    sent_ref = sent_blocks.reshape(OWNERS * TILES * CAP, LANES)
    width = 8 * SPAN * CAP
    strips = [pl.ds(strip * width, width) for strip in range(TILES // (8 * SPAN))]
    loads = [
        pltpu.make_async_copy(held_out_ref.at[:, rows], held_blocks.at[:, rows], held_sems.at[strip])
        for strip, rows in enumerate(strips)
    ]
    stores = [
        pltpu.make_async_copy(sent_blocks.at[:, rows], sent_out_ref.at[:, rows], sent_sems.at[strip])
        for strip, rows in enumerate(strips)
    ]
    for load in loads:
        load.start()
    table = strain_tables(
        low_ref[...], high_ref[...], fraction_ref[...], matrix_ref[...], scale_ref[...]
    )
    for step in range(NSUB):
        levels_ref[pl.ds(step * POINTS, POINTS), :] = table[:, step * LANES : (step + 1) * LANES]
    sent_blocks[...] = jnp.zeros_like(sent_blocks)
    for strip in range(len(strips)):
        loads[strip].wait()
        parts = [SPAN * strip + part for part in range(SPAN)]
        codes = [codes_ref[pl.ds(8 * part, 8), :] for part in parts]
        flow = [flow_ref[pl.ds(8 * part, 8), :] * (1.0 / (young + harden)) for part in parts]
        floor = [-limit for limit in flow]
        for steps in range(1, NSUB + 1):
            first = plan_ref[3 * LISTED + steps - 1]
            end = plan_ref[3 * LISTED + steps]
            gains = []
            for part in parts:
                rate = rate_ref[pl.ds(8 * part, 8), :] * ((young + harden) / steps)
                gains.append(rate / (1.0 + rate))

            def advance(
                place, count, steps=steps, gains=gains, parts=parts, codes=codes, flow=flow, floor=floor
            ):
                elements = [plan_ref[place + i] for i in range(count)]
                sources = [plan_ref[LISTED + place + i] for i in range(count)]
                state = [
                    [held_ref[row_part(source, part), :] for part in parts]
                    for source in sources
                ]
                for start in range(0, count, 4):
                    for step in range(steps):
                        for i in range(start, start + 4):
                            level = jnp.broadcast_to(
                                levels_ref[pl.ds(step * POINTS + elements[i], 1), :],
                                (8, LANES),
                            )
                            for part in range(SPAN):
                                stress = jnp.take_along_axis(level, codes[part], axis=1)
                                trial = stress - state[i][part]
                                held = jnp.minimum(jnp.maximum(trial, floor[part]), flow[part])
                                state[i][part] = state[i][part] + (trial - held) * gains[part]
                targets = [plan_ref[2 * LISTED + place + i] for i in range(count)]
                for i in range(count):
                    for part in range(SPAN):
                        sent_ref[row_part(targets[i], parts[part]), :] = state[i][part]

            groups = (end - first) // GROUP

            def pair(turn, carry, first=first, advance=advance):
                advance(first + 2 * GROUP * turn, 2 * GROUP)
                return carry

            def single(turn, carry, first=first, advance=advance):
                advance(first + GROUP * turn, GROUP)
                return carry

            lax.fori_loop(0, groups // 2, pair, 0)
            lax.fori_loop(groups // 2 * 2, groups, single, 0)
        stores[strip].start()
    for store in stores:
        store.wait()


def relax(order, low, high, fraction, codes, flow, rate, held):
    smem = pl.BlockSpec(memory_space=pltpu.SMEM)
    vmem = pl.BlockSpec(memory_space=pltpu.VMEM)
    outside = pl.BlockSpec(memory_space=pl.ANY)
    strips = TILES // (8 * SPAN)
    matrix, scale = table_matrix()
    return pl.pallas_call(
        relax_kernel,
        out_shape=jax.ShapeDtypeStruct(held.shape, jnp.float32),
        in_specs=[smem] + [vmem] * 8 + [outside],
        out_specs=outside,
        scratch_shapes=[
            pltpu.VMEM((NSUB * POINTS, LANES), jnp.float32),
            pltpu.VMEM(held.shape, jnp.float32),
            pltpu.VMEM(held.shape, jnp.float32),
            pltpu.SemaphoreType.DMA((strips,)),
            pltpu.SemaphoreType.DMA((strips,)),
        ],
        compiler_params=pltpu.CompilerParams(vmem_limit_bytes=VMEM_LIMIT),
        name="relax",
    )(
        order,
        low,
        high,
        fraction,
        jnp.asarray(matrix, jnp.bfloat16),
        jnp.asarray(scale),
        codes,
        flow,
        rate,
        held,
    )


def stress_kernel(plan_ref, codes_ref, last_ref, basis_ref, sent_ref, sums_ref):
    def one(place, carry):
        element = plan_ref[place]
        target = plan_ref[2 * LISTED + place]
        level = jnp.broadcast_to(last_ref[pl.ds(element, 1), :], (8, LANES))
        totals = [None] * 6
        for quad in range(TILES // 8):
            stress = jnp.take_along_axis(level, codes_ref[pl.ds(8 * quad, 8), :], axis=1)
            stress = stress - young * sent_ref[row_part(target, quad), :]
            for part in range(6):
                term = stress * basis_ref[pl.ds(part * TILES + 8 * quad, 8), :]
                totals[part] = term if quad == 0 else totals[part] + term
        for part in range(6):
            sums_ref[pl.ds(part * POINTS + element, 1), :] = jnp.sum(
                totals[part], axis=0, keepdims=True
            )
        return carry

    lax.fori_loop(0, plan_ref[3 * LISTED + NSUB], one, 0)


def cell_stress(order, codes, last, basis, sent):
    smem = pl.BlockSpec(memory_space=pltpu.SMEM)
    vmem = pl.BlockSpec(memory_space=pltpu.VMEM)
    sums = pl.pallas_call(
        stress_kernel,
        out_shape=jax.ShapeDtypeStruct((6 * POINTS, LANES), jnp.float32),
        in_specs=[smem] + [vmem] * 4,
        out_specs=vmem,
        compiler_params=pltpu.CompilerParams(vmem_limit_bytes=32 * 2**20),
        name="cell_stress",
    )(order, codes, last, basis, sent.reshape(OWNERS * TILES * CAP, LANES))
    return jnp.sum(sums, axis=1).reshape(6, POINTS) / STRUTS


def hand_over(slots):
    pieces = 4
    height = slots.shape[0] // pieces

    def kernel(received_ref, result_ref, buffer, in_sems, out_sems):
        loads, stores = [], []
        for piece in range(pieces):
            rows = pl.ds(piece * height, height)
            loads.append(
                pltpu.make_async_copy(received_ref.at[rows], buffer.at[rows], in_sems.at[piece])
            )
            stores.append(
                pltpu.make_async_copy(buffer.at[rows], result_ref.at[rows], out_sems.at[piece])
            )
        for load in loads:
            load.start()
        for load, store in zip(loads, stores):
            load.wait()
            store.start()
        for store in stores:
            store.wait()

    outside = pl.BlockSpec(memory_space=pl.ANY)
    return pl.pallas_call(
        kernel,
        out_shape=jax.ShapeDtypeStruct(slots.shape, slots.dtype),
        in_specs=[outside],
        out_specs=outside,
        scratch_shapes=[
            pltpu.VMEM(slots.shape, slots.dtype),
            pltpu.SemaphoreType.DMA((pieces,)),
            pltpu.SemaphoreType.DMA((pieces,)),
        ],
        compiler_params=pltpu.CompilerParams(vmem_limit_bytes=VMEM_LIMIT),
        name="hand_over",
    )(slots)


def to_tiles(slots):
    split = slots.reshape(OWNERS, CAP, TILES, LANES)
    return split.transpose(0, 2, 1, 3).reshape(OWNERS, TILES * CAP, LANES)


def from_tiles(tiles):
    split = tiles.reshape(OWNERS, TILES, CAP, LANES)
    return split.transpose(0, 2, 1, 3).reshape(OWNERS * CAP, STRUTS)


def exchange(blocks):
    return lax.all_to_all(blocks, "rve", split_axis=0, concat_axis=0, tiled=True)


def shards(
    displacement,
    velocity,
    old_owner,
    new_owner,
    substeps,
    strut_ends,
    flow_stress,
    relax_rate,
    plastic_old,
):
    planes = displacement.shape[1]
    held = exchange(to_tiles(plastic_old))

    displacement_next = displacement + time_step * velocity
    low = jnp.concatenate([displacement, displacement_next], axis=0).reshape(6, LANES)
    low = jnp.pad(low, ((0, 2), (0, 0)))
    order, low = plan(old_owner.reshape(-1), new_owner.reshape(-1), substeps, low)
    high = from_behind(low, ("macro", "rve"), -1)
    codes = direction_codes(strut_ends)
    counts = substeps.astype(jnp.float32)
    turns = jnp.arange(1, NSUB + 1, dtype=jnp.float32)[:, None]
    fraction = jnp.minimum(turns, counts[None, :]) / counts[None, :]
    flow = flow_stress.reshape(TILES, LANES)
    rate = relax_rate.reshape(TILES, LANES)
    sent = relax(order, low, high, fraction, codes, flow, rate, held)

    plastic_new = hand_over(from_tiles(exchange(sent)))

    products = jnp.asarray(direction_products())
    doubled = jnp.asarray(np.array([1, 1, 1, 2, 2, 2], np.float32))[:, None] * products
    rim_next = high[3:6].reshape(displacement.shape)
    deform_new = element_deform(jnp.concatenate([displacement_next, rim_next], axis=1))
    last = young * jnp.einsum("ce,cd->ed", green(deform_new), doubled, precision=highest)
    basis = jnp.take(products, codes.reshape(-1), axis=1).reshape(6 * TILES, LANES)
    stress = cell_stress(order, codes, last, basis, sent)
    piola = first_stress(deform_new, stress)
    nodal = nodal_force(piola, (planes, displacement.shape[2], displacement.shape[3]))
    carried = from_behind(nodal[:, planes:], ("macro", "rve"), 1)
    interior = nodal[:, :planes].at[:, :1].add(carried)
    velocity_next = velocity - time_step * interior
    return (displacement_next, velocity_next, plastic_new)


def solution(mesh):
    in_specs = (
        P(None, ("macro", "rve"), None, None),
        P(None, ("macro", "rve"), None, None),
        P(("macro", "rve"), None),
        P(("macro", "rve"), None),
        P(("macro", "rve")),
        P(),
        P(),
        P(),
        P(("macro", "rve"), None),
    )
    out_specs = (
        P(None, ("macro", "rve"), None, None),
        P(None, ("macro", "rve"), None, None),
        P(("macro", "rve"), None),
    )
    return jax.shard_map(shards, mesh=mesh, in_specs=in_specs, out_specs=out_specs, check_vma=False)
```

```python
import functools

import jax
import jax.numpy as jnp
import numpy as np
from jax import lax
from jax.experimental import pallas as pl
from jax.experimental.pallas import tpu as pltpu
from jax.sharding import PartitionSpec as P

STRUTS = 4096
NSUB = 8
LATTICE = 8
LANES = 128
POINTS = 128
TILES = STRUTS // LANES
EZ = 16
OWNERS = 32
CAP = 8
GROUP = 8
SPAN = 2
LISTED = 192
VMEM_LIMIT = 60 * 2**20

young = 10.0
harden = 1.0
time_step = 0.2
highest = lax.Precision.HIGHEST


def from_behind(value, axis, steps):
    count = lax.axis_size(axis)
    initial, last = (max(0, -steps), min(count, count - steps))
    return lax.ppermute(value, axis, [(source, source + steps) for source in range(initial, last)])


def direction_products():
    table = np.zeros((6, LANES), np.float32)
    for code in range(27):
        vector = np.array([code // 9 - 1, code // 3 % 3 - 1, code % 3 - 1], np.float32)
        length = np.sqrt(np.sum(vector * vector, dtype=np.float32))
        if length == 0:
            continue
        x, y, z = vector / length
        table[:, code] = [x * x, y * y, z * z, x * y, x * z, y * z]
    return table


def table_matrix():
    steps_of = np.zeros((6, LANES), np.float32)
    scale = np.zeros((1, LANES), np.float32)
    for code in range(27):
        x, y, z = (code // 9 - 1, code // 3 % 3 - 1, code % 3 - 1)
        length = x * x + y * y + z * z
        if length == 0:
            continue
        steps_of[:, code] = [x * x, y * y, z * z, 2 * x * y, 2 * x * z, 2 * y * z]
        scale[0, code] = young / (young + harden) / length
    matrix = np.zeros((3, 6, NSUB, NSUB, LANES), np.float32)
    for step in range(NSUB):
        matrix[:, :, step, step] = steps_of
    return matrix.reshape(3 * 6 * NSUB, NSUB * LANES), np.tile(scale, (1, NSUB))


def direction_codes(strut_ends):
    first, second = strut_ends[0], strut_ends[1]

    def step(scale):
        offset = second // scale % LATTICE - first // scale % LATTICE
        return (offset + LATTICE // 2) % LATTICE - LATTICE // 2

    code = (step(LATTICE * LATTICE) + 1) * 9 + (step(LATTICE) + 1) * 3 + (step(1) + 1)
    return code.reshape(TILES, LANES)


def green(deform, stacked=True):

    def column_dot(col_a, col_b):
        return (
            deform[col_a] * deform[col_b]
            + deform[3 + col_a] * deform[3 + col_b]
            + deform[6 + col_a] * deform[6 + col_b]
        )

    strain = [
        0.5 * (column_dot(0, 0) - 1.0),
        0.5 * (column_dot(1, 1) - 1.0),
        0.5 * (column_dot(2, 2) - 1.0),
        0.5 * column_dot(0, 1),
        0.5 * column_dot(0, 2),
        0.5 * column_dot(1, 2),
    ]
    return jnp.stack(strain) if stacked else strain


def first_stress(deform, stress):
    pairing = ((0, 3, 4), (3, 1, 5), (4, 5, 2))
    components = []
    for row_axis in range(3):
        for col_axis in range(3):
            components.append(
                deform[3 * row_axis] * stress[pairing[0][col_axis]]
                + deform[3 * row_axis + 1] * stress[pairing[1][col_axis]]
                + deform[3 * row_axis + 2] * stress[pairing[2][col_axis]]
            )
    return jnp.stack(components)


def element_deform(extended):
    plane_low = extended[:, :-1]
    plane_high = extended[:, 1:]

    def roll_second(values):
        return jnp.roll(values, -1, axis=2)

    def roll_third(values):
        return jnp.roll(values, -1, axis=3)

    diff_first = plane_high - plane_low
    slope_first = 0.25 * (
        diff_first
        + roll_second(diff_first)
        + roll_third(diff_first)
        + roll_second(roll_third(diff_first))
    )
    plane_mid = 0.5 * (plane_low + plane_high)
    diff_second = roll_second(plane_mid) - plane_mid
    slope_second = 0.5 * (diff_second + roll_third(diff_second))
    diff_third = roll_third(plane_mid) - plane_mid
    slope_third = 0.5 * (diff_third + roll_second(diff_third))
    slopes = jnp.stack([slope_first, slope_second, slope_third], axis=1)
    identity = jnp.eye(3, dtype=extended.dtype)
    slopes = slopes + identity[:, :, None, None, None]
    return slopes.reshape(9, -1)


def nodal_force(piola, layout):
    tensor = piola.reshape((3, 3) + layout)
    planes = layout[0]
    nodal = jnp.zeros((3, planes + 1, layout[1], layout[2]), piola.dtype)
    for offset_plane in (0, 1):
        for offset_row in (0, 1):
            for offset_col in (0, 1):
                corner_term = 0.25 * (
                    (2 * offset_plane - 1) * tensor[:, 0]
                    + (2 * offset_row - 1) * tensor[:, 1]
                    + (2 * offset_col - 1) * tensor[:, 2]
                )
                corner_term = jnp.roll(
                    jnp.roll(corner_term, offset_row, axis=2), offset_col, axis=3
                )
                nodal = nodal.at[:, offset_plane : offset_plane + planes].add(corner_term)
    return nodal


def plan_kernel(old_ref, new_ref, steps_ref, planes_ref, plan_ref, handed_ref, seen_ref):
    handed_ref[...] = planes_ref[...]

    def clear(index, carry):
        seen_ref[index] = 0
        return carry

    lax.fori_loop(0, 2 * OWNERS + NSUB + 1, clear, 0)

    def count(element, carry):
        level = 2 * OWNERS + steps_ref[element]
        seen_ref[level] = seen_ref[level] + 1
        return carry

    lax.fori_loop(0, POINTS, count, 0)
    start = 0
    for steps in range(NSUB + 1):
        held = seen_ref[2 * OWNERS + steps]
        seen_ref[2 * OWNERS + steps] = start
        start = start + (held + GROUP - 1) // GROUP * GROUP
        plan_ref[3 * LISTED + steps] = start

    def place(element, carry):
        old = old_ref[element]
        old_rank = seen_ref[old]
        seen_ref[old] = old_rank + 1
        new = OWNERS + new_ref[element]
        new_rank = seen_ref[new]
        seen_ref[new] = new_rank + 1
        level = 2 * OWNERS + steps_ref[element]
        position = seen_ref[level]
        seen_ref[level] = position + 1
        plan_ref[position] = element
        plan_ref[LISTED + position] = old * (TILES * CAP) + old_rank
        plan_ref[2 * LISTED + position] = (new - OWNERS) * (TILES * CAP) + new_rank
        return carry

    lax.fori_loop(0, POINTS, place, 0)
    for steps in range(1, NSUB + 1):
        filled = seen_ref[2 * OWNERS + steps]

        def repeat(position, carry, filled=filled):
            for part in range(3):
                plan_ref[part * LISTED + position] = plan_ref[part * LISTED + filled - 1]
            return carry

        lax.fori_loop(filled, plan_ref[3 * LISTED + steps], repeat, 0)


def plan(old_owner, new_owner, substeps, planes):
    smem = pl.BlockSpec(memory_space=pltpu.SMEM)
    vmem = pl.BlockSpec(memory_space=pltpu.VMEM)
    return pl.pallas_call(
        plan_kernel,
        out_shape=(
            jax.ShapeDtypeStruct((4 * LISTED,), jnp.int32),
            jax.ShapeDtypeStruct(planes.shape, planes.dtype),
        ),
        in_specs=[smem] * 3 + [vmem],
        out_specs=(smem, vmem),
        scratch_shapes=[pltpu.SMEM((2 * OWNERS + NSUB + 1,), jnp.int32)],
        name="plan",
    )(old_owner, new_owner, substeps, planes)


def row_part(row, part):
    return pl.ds(row + 8 * CAP * part, 8, stride=CAP)


def next_row(values):
    return pltpu.roll(values, LANES - EZ, 1)


def next_col(values):
    lane = lax.broadcasted_iota(jnp.int32, values.shape, 1)
    return jnp.where(
        lane % EZ == EZ - 1, pltpu.roll(values, EZ - 1, 1), pltpu.roll(values, LANES - 1, 1)
    )


def strain_tables(low, high, fraction, matrix, scale):
    rise = high - low
    middle = 0.5 * (low + high)
    rise = rise + next_col(rise)
    along_row = next_row(middle) - middle
    along_col = next_col(middle) - middle
    slopes = [
        0.25 * (rise + next_row(rise)),
        0.5 * (along_row + next_col(along_row)),
        0.5 * (along_col + next_row(along_col)),
    ]
    path = []
    for row in range(3):
        for col in range(3):
            unit = 1.0 if row == col else 0.0
            old = slopes[col][row : row + 1] + unit
            new = slopes[col][3 + row : 4 + row] + unit
            path.append(
                jnp.broadcast_to(old, (NSUB, LANES))
                + fraction * jnp.broadcast_to(new - old, (NSUB, LANES))
            )
    strain = green(path, False)
    addends = []
    for _ in range(3):
        rounded = [part.astype(jnp.bfloat16).astype(jnp.float32) for part in strain]
        strain = [part - near for part, near in zip(strain, rounded)]
        addends += rounded
    addends = jnp.concatenate(addends, axis=0).astype(jnp.bfloat16)
    table = lax.dot_general(
        addends, matrix, (((0,), (0,)), ((), ())), preferred_element_type=jnp.float32
    )
    return table * scale


def relax_kernel(
    plan_ref,
    low_ref,
    high_ref,
    fraction_ref,
    matrix_ref,
    scale_ref,
    codes_ref,
    flow_ref,
    rate_ref,
    held_out_ref,
    sent_out_ref,
    levels_ref,
    held_blocks,
    sent_blocks,
    held_sems,
    sent_sems,
):
    held_ref = held_blocks.reshape(OWNERS * TILES * CAP, LANES)
    sent_ref = sent_blocks.reshape(OWNERS * TILES * CAP, LANES)
    width = 8 * SPAN * CAP
    strips = [pl.ds(strip * width, width) for strip in range(TILES // (8 * SPAN))]
    loads = [
        pltpu.make_async_copy(held_out_ref.at[:, rows], held_blocks.at[:, rows], held_sems.at[strip])
        for strip, rows in enumerate(strips)
    ]
    stores = [
        pltpu.make_async_copy(sent_blocks.at[:, rows], sent_out_ref.at[:, rows], sent_sems.at[strip])
        for strip, rows in enumerate(strips)
    ]
    loads[0].start()
    table = strain_tables(
        low_ref[...], high_ref[...], fraction_ref[...], matrix_ref[...], scale_ref[...]
    )
    for step in range(NSUB):
        levels_ref[pl.ds(step * POINTS, POINTS), :] = table[:, step * LANES : (step + 1) * LANES]
    sent_blocks[...] = jnp.zeros_like(sent_blocks)
    for strip in range(len(strips)):
        loads[strip].wait()
        if strip + 1 < len(strips):
            loads[strip + 1].start()
        parts = [SPAN * strip + part for part in range(SPAN)]
        codes = [codes_ref[pl.ds(8 * part, 8), :] for part in parts]
        flow = [flow_ref[pl.ds(8 * part, 8), :] * (1.0 / (young + harden)) for part in parts]
        floor = [-limit for limit in flow]
        for steps in range(1, NSUB + 1):
            first = plan_ref[3 * LISTED + steps - 1]
            end = plan_ref[3 * LISTED + steps]
            gains = []
            for part in parts:
                rate = rate_ref[pl.ds(8 * part, 8), :] * ((young + harden) / steps)
                gains.append(rate / (1.0 + rate))

            def advance(
                place, count, steps=steps, gains=gains, parts=parts, codes=codes, flow=flow, floor=floor
            ):
                elements = [plan_ref[place + i] for i in range(count)]
                sources = [plan_ref[LISTED + place + i] for i in range(count)]
                state = [
                    [held_ref[row_part(source, part), :] for part in parts]
                    for source in sources
                ]
                for start in range(0, count, 4):
                    for step in range(steps):
                        for i in range(start, start + 4):
                            level = jnp.broadcast_to(
                                levels_ref[pl.ds(step * POINTS + elements[i], 1), :],
                                (8, LANES),
                            )
                            for part in range(SPAN):
                                stress = jnp.take_along_axis(level, codes[part], axis=1)
                                trial = stress - state[i][part]
                                held = jnp.minimum(jnp.maximum(trial, floor[part]), flow[part])
                                state[i][part] = state[i][part] + (trial - held) * gains[part]
                targets = [plan_ref[2 * LISTED + place + i] for i in range(count)]
                for i in range(count):
                    for part in range(SPAN):
                        sent_ref[row_part(targets[i], parts[part]), :] = state[i][part]

            groups = (end - first) // GROUP

            def pair(turn, carry, first=first, advance=advance):
                advance(first + 2 * GROUP * turn, 2 * GROUP)
                return carry

            def single(turn, carry, first=first, advance=advance):
                advance(first + GROUP * turn, GROUP)
                return carry

            lax.fori_loop(0, groups // 2, pair, 0)
            lax.fori_loop(groups // 2 * 2, groups, single, 0)
        stores[strip].start()
    for store in stores:
        store.wait()


def relax(order, low, high, fraction, codes, flow, rate, held):
    smem = pl.BlockSpec(memory_space=pltpu.SMEM)
    vmem = pl.BlockSpec(memory_space=pltpu.VMEM)
    outside = pl.BlockSpec(memory_space=pl.ANY)
    strips = TILES // (8 * SPAN)
    matrix, scale = table_matrix()
    return pl.pallas_call(
        relax_kernel,
        out_shape=jax.ShapeDtypeStruct(held.shape, jnp.float32),
        in_specs=[smem] + [vmem] * 8 + [outside],
        out_specs=outside,
        scratch_shapes=[
            pltpu.VMEM((NSUB * POINTS, LANES), jnp.float32),
            pltpu.VMEM(held.shape, jnp.float32),
            pltpu.VMEM(held.shape, jnp.float32),
            pltpu.SemaphoreType.DMA((strips,)),
            pltpu.SemaphoreType.DMA((strips,)),
        ],
        compiler_params=pltpu.CompilerParams(vmem_limit_bytes=VMEM_LIMIT),
        name="relax",
    )(
        order,
        low,
        high,
        fraction,
        jnp.asarray(matrix, jnp.bfloat16),
        jnp.asarray(scale),
        codes,
        flow,
        rate,
        held,
    )


def stress_kernel(plan_ref, codes_ref, last_ref, basis_ref, sent_ref, sums_ref):
    def one(place, carry):
        element = plan_ref[place]
        target = plan_ref[2 * LISTED + place]
        level = jnp.broadcast_to(last_ref[pl.ds(element, 1), :], (8, LANES))
        totals = [None] * 6
        for quad in range(TILES // 8):
            stress = jnp.take_along_axis(level, codes_ref[pl.ds(8 * quad, 8), :], axis=1)
            stress = stress - young * sent_ref[row_part(target, quad), :]
            for part in range(6):
                term = stress * basis_ref[pl.ds(part * TILES + 8 * quad, 8), :]
                totals[part] = term if quad == 0 else totals[part] + term
        for part in range(6):
            sums_ref[pl.ds(part * POINTS + element, 1), :] = jnp.sum(
                totals[part], axis=0, keepdims=True
            )
        return carry

    lax.fori_loop(0, plan_ref[3 * LISTED + NSUB], one, 0)


def cell_stress(order, codes, last, basis, sent):
    smem = pl.BlockSpec(memory_space=pltpu.SMEM)
    vmem = pl.BlockSpec(memory_space=pltpu.VMEM)
    sums = pl.pallas_call(
        stress_kernel,
        out_shape=jax.ShapeDtypeStruct((6 * POINTS, LANES), jnp.float32),
        in_specs=[smem] + [vmem] * 4,
        out_specs=vmem,
        compiler_params=pltpu.CompilerParams(vmem_limit_bytes=32 * 2**20),
        name="cell_stress",
    )(order, codes, last, basis, sent.reshape(OWNERS * TILES * CAP, LANES))
    return jnp.sum(sums, axis=1).reshape(6, POINTS) / STRUTS


def hand_over(slots):
    heights = (16, 48, 64, 64, 48, 16)
    pieces = len(heights)

    def kernel(received_ref, result_ref, buffer, in_sems, out_sems):
        loads, stores = [], []
        for piece in range(pieces):
            rows = pl.ds(sum(heights[:piece]), heights[piece])
            loads.append(
                pltpu.make_async_copy(received_ref.at[rows], buffer.at[rows], in_sems.at[piece])
            )
            stores.append(
                pltpu.make_async_copy(buffer.at[rows], result_ref.at[rows], out_sems.at[piece])
            )
        for load in loads:
            load.start()
        for load, store in zip(loads, stores):
            load.wait()
            store.start()
        for store in stores:
            store.wait()

    outside = pl.BlockSpec(memory_space=pl.ANY)
    return pl.pallas_call(
        kernel,
        out_shape=jax.ShapeDtypeStruct(slots.shape, slots.dtype),
        in_specs=[outside],
        out_specs=outside,
        scratch_shapes=[
            pltpu.VMEM(slots.shape, slots.dtype),
            pltpu.SemaphoreType.DMA((pieces,)),
            pltpu.SemaphoreType.DMA((pieces,)),
        ],
        compiler_params=pltpu.CompilerParams(vmem_limit_bytes=VMEM_LIMIT),
        name="hand_over",
    )(slots)


def to_tiles(slots):
    split = slots.reshape(OWNERS, CAP, TILES, LANES)
    return split.transpose(0, 2, 1, 3).reshape(OWNERS, TILES * CAP, LANES)


def from_tiles(tiles):
    split = tiles.reshape(OWNERS, TILES, CAP, LANES)
    return split.transpose(0, 2, 1, 3).reshape(OWNERS * CAP, STRUTS)


def exchange(blocks):
    return lax.all_to_all(blocks, "rve", split_axis=0, concat_axis=0, tiled=True)


def shards(
    displacement,
    velocity,
    old_owner,
    new_owner,
    substeps,
    strut_ends,
    flow_stress,
    relax_rate,
    plastic_old,
):
    planes = displacement.shape[1]
    held = exchange(to_tiles(plastic_old))

    displacement_next = displacement + time_step * velocity
    low = jnp.concatenate([displacement, displacement_next], axis=0).reshape(6, LANES)
    low = jnp.pad(low, ((0, 2), (0, 0)))
    order, low = plan(old_owner.reshape(-1), new_owner.reshape(-1), substeps, low)
    high = from_behind(low, ("macro", "rve"), -1)
    codes = direction_codes(strut_ends)
    counts = substeps.astype(jnp.float32)
    turns = jnp.arange(1, NSUB + 1, dtype=jnp.float32)[:, None]
    fraction = jnp.minimum(turns, counts[None, :]) / counts[None, :]
    flow = flow_stress.reshape(TILES, LANES)
    rate = relax_rate.reshape(TILES, LANES)
    sent = relax(order, low, high, fraction, codes, flow, rate, held)

    plastic_new = hand_over(from_tiles(exchange(sent)))

    products = jnp.asarray(direction_products())
    doubled = jnp.asarray(np.array([1, 1, 1, 2, 2, 2], np.float32))[:, None] * products
    rim_next = high[3:6].reshape(displacement.shape)
    deform_new = element_deform(jnp.concatenate([displacement_next, rim_next], axis=1))
    last = young * jnp.einsum("ce,cd->ed", green(deform_new), doubled, precision=highest)
    basis = jnp.take(products, codes.reshape(-1), axis=1).reshape(6 * TILES, LANES)
    stress = cell_stress(order, codes, last, basis, sent)
    piola = first_stress(deform_new, stress)
    nodal = nodal_force(piola, (planes, displacement.shape[2], displacement.shape[3]))
    carried = from_behind(nodal[:, planes:], ("macro", "rve"), 1)
    interior = nodal[:, :planes].at[:, :1].add(carried)
    velocity_next = velocity - time_step * interior
    return (displacement_next, velocity_next, plastic_new)


def solution(mesh):
    in_specs = (
        P(None, ("macro", "rve"), None, None),
        P(None, ("macro", "rve"), None, None),
        P(("macro", "rve"), None),
        P(("macro", "rve"), None),
        P(("macro", "rve")),
        P(),
        P(),
        P(),
        P(("macro", "rve"), None),
    )
    out_specs = (
        P(None, ("macro", "rve"), None, None),
        P(None, ("macro", "rve"), None, None),
        P(("macro", "rve"), None),
    )
    return jax.shard_map(shards, mesh=mesh, in_specs=in_specs, out_specs=out_specs, check_vma=False)
```
